32 devices in a mesh: seg: 8 (over z, y), grp: 4 (over x, core).
Axes of the slice: x: 2, y: 2, z: 4, core: 2. Of those that a mesh axis runs over, the one named last changes fastest.
Arguments:
- basis: float32 [8, 768, 128], P(None, ('seg', 'grp')), may hold values from -6 to 6
- coords: float32 [768, 3, 128], P(('seg', 'grp')), may hold values from 0 to 4
- areas: float32 [768, 128], P(('seg', 'grp')), may hold values from 0.5 to 2
- p2m: bfloat16 [768, 121, 128], P(('seg', 'grp')), may hold values from -0.5 to 0.5
- l2p: bfloat16 [768, 128, 121], P(('seg', 'grp')), may hold values from -0.5 to 0.5
- m2l: bfloat16 [316, 121, 121], replicated, may hold values from -0.0390625 to 0.0390625
- counts: int32 [32], P(('seg', 'grp')), may hold values from 8 to 24
- near_list: int32 [768, 27], P(('seg', 'grp')), may hold values from 0 to 287
- far_list: int32 [768, 189], P(('seg', 'grp')), may hold values from 0 to 287
- far_offset: int32 [768, 189], P(('seg', 'grp')), may hold values from 0 to 315
Outputs:
- new_vector: float32 [768, 128], P(('seg', 'grp'))
- hessenberg: float32 [9], replicated
The draws below stay inside these ranges and needn't reach their ends.
Inputs may be any that keep to these rules, and one draw needn't show every extreme that they name: `near_list`: window indices follow the rule of the steps; entries may name empty slots or leaves beyond the ends of the curve, which contribute nothing. A device's live leaves are its first counts slots.
All inputs are finite; a program needn't handle non-finite values.
Results may differ from the reference program's by a relative error of at most 0.0012.
Values sent between devices are 32-bit elements; how exact they have to be, the bound alone decides.
No kernel may reach another device: no remote copies, remote signals or barrier semaphores. Data moves between devices by JAX's collectives and lax.ppermute only.
A program may use at most 64 MiB of HBM per device.

```python
import math
import jax
import jax.numpy as jnp
from jax import lax

PAN = 128
TERMS = 121
OFFSETS = 316
FAR = 189
NEAR = 27
KRYLOV = 8
LEAF_DEV = 24
LEAVES = 768
N_SEG = 8
N_GRP = 4


def draw_basis(key, part):
    first, second = jax.random.split(jax.random.fold_in(key, 17))
    separate = jnp.clip(jax.random.normal(first, (KRYLOV, LEAVES, PAN), jnp.float32), -4.0, 4.0)
    shared = jnp.clip(jax.random.normal(second, (1, LEAVES, PAN), jnp.float32), -4.0, 4.0)
    return 0.6 * separate + 0.8 * shared


def place_ends(entries, own_key, least, high):
    dims = entries.shape
    spot = [jax.random.randint(jax.random.fold_in(own_key, axis), (), 0, dims[axis]) for axis in range(len(dims))]
    entries = entries.at[tuple(spot)].set(least)
    longest = dims.index(max(dims))
    spot[longest] = (spot[longest] + 1) % dims[longest]
    return entries.at[tuple(spot)].set(high)


def steps_of(own_key, shape, cuts, smallest, top_value):
    def one(axis_at, parts):
        draws = jax.random.uniform(jax.random.fold_in(jax.random.fold_in(own_key, 6), axis_at), (parts,), jnp.float32, smallest / len(cuts), top_value / len(cuts))
        return jnp.repeat(jnp.exp(draws), shape[axis_at] // parts).reshape((-1,) + (1,) * (len(shape) - axis_at - 1))

    factor_of = one(*cuts[0])
    for cut in cuts[1:]:
        factor_of = factor_of * one(*cut)
    return factor_of


def bell_draw(rng, shape, scale, reach, shards=(), kind=jnp.bfloat16):
    result = scale * jax.random.normal(rng, shape, jnp.float32)
    if shards:
        result = result * steps_of(rng, shape, shards, -0.22, 0.18)
    return jnp.clip(result, -reach, reach).astype(kind)


def setup_inputs(seed: int = 0) -> dict:
    splits = jax.random.split(jax.random.key(seed), 11)
    basis = draw_basis(jax.random.fold_in(splits[10], 71), 0)
    coords = jnp.clip(4.0 * jax.random.uniform(splits[1], (LEAVES, 3, PAN), jnp.float32) ** steps_of(splits[1], (LEAVES, 3, PAN), ((0, 32),), -0.2, 0.2), 0.0, 4.0)
    areas = jnp.clip(jnp.exp(math.log(2.0) - 1.3862944 * jax.random.uniform(splits[2], (LEAVES, PAN), jnp.float32) ** steps_of(splits[2], (LEAVES, PAN), ((0, 32),), -0.2, 0.2)), 0.5, 2.0)
    p2m = bell_draw(splits[3], (LEAVES, TERMS, PAN), PAN ** -0.5, 0.5, ((0, 32),))
    l2p = bell_draw(splits[4], (LEAVES, PAN, TERMS), TERMS ** -0.5, 0.5, ((0, 32),))
    m2l = bell_draw(splits[5], (OFFSETS, TERMS, TERMS), (TERMS * FAR) ** -0.5, 0.0390625)
    counts = place_ends(jax.random.randint(splits[6], (N_SEG * N_GRP,), LEAF_DEV // 3, LEAF_DEV + 1), jax.random.fold_in(splits[6], 1), LEAF_DEV // 3, LEAF_DEV).astype(jnp.int32)
    near_list = place_ends(jax.random.randint(splits[7], (LEAVES, NEAR), 0, 3 * N_GRP * LEAF_DEV), jax.random.fold_in(splits[7], 1), 0, (3 * N_GRP * LEAF_DEV) - 1).astype(jnp.int32)
    far_list = place_ends(jax.random.randint(splits[8], (LEAVES, FAR), 0, 3 * N_GRP * LEAF_DEV), jax.random.fold_in(splits[8], 1), 0, (3 * N_GRP * LEAF_DEV) - 1).astype(jnp.int32)
    far_offset = place_ends(jax.random.randint(splits[9], (LEAVES, FAR), 0, OFFSETS), jax.random.fold_in(splits[9], 1), 0, OFFSETS - 1).astype(jnp.int32)
    return {"basis": basis, "coords": coords, "areas": areas, "p2m": p2m, "l2p": l2p, "m2l": m2l, "counts": counts, "near_list": near_list, "far_list": far_list, "far_offset": far_offset}


four_pi = 12.566370614359172
epsilon = 1e-06
highest = lax.Precision.HIGHEST

def live_slots(counts, leaves):
    leaf_dev = leaves // counts.shape[0]
    position = jnp.arange(leaves, dtype=jnp.int32)
    owner = position // leaf_dev
    return (position % leaf_dev < counts[owner]).astype(jnp.float32)[:, None]

def reference(basis, coords, areas, p2m, l2p, m2l, counts, near_list, far_list, far_offset):
    leaves, panels = areas.shape
    krylov = basis.shape[0]
    terms = m2l.shape[1]
    offsets = m2l.shape[0]
    far_count = far_list.shape[1]
    group = N_GRP * (leaves // counts.shape[0])
    live_mask = live_slots(counts, leaves)
    current = basis[krylov - 1] * live_mask
    rounded = current.astype(jnp.bfloat16)
    rounded = lax.optimization_barrier(rounded)
    multipoles = jnp.einsum('lkp,lp->lk', p2m.astype(jnp.float32), rounded.astype(jnp.float32), precision=highest)
    packed = jnp.concatenate([coords, areas[:, None, :], current[:, None, :]], axis=1)
    padded = jnp.pad(packed, ((group, group), (0, 0), (0, 0)))
    poles = jnp.pad(multipoles, ((group, group), (0, 0)))
    base_index = (jnp.arange(leaves, dtype=jnp.int32) // group * group)[:, None]
    near_rows = (base_index + near_list).astype(jnp.int32)
    far_rows = (base_index + far_list).astype(jnp.int32)
    table = m2l.astype(jnp.float32)

    def segment_work(leaf_block):
        target, near_block, far_block, offset_block = leaf_block

        def near_step(running, column):
            source = padded[column]
            square = jnp.zeros((group, panels, panels), jnp.float32)
            for component in range(3):
                spread = target[:, component, :, None] - source[:, component, None, :]
                square = square + spread * spread
            source_area = source[:, 3, None, :]
            kernel = source_area / (four_pi * jnp.sqrt(square + source_area))
            return (running + lax.optimization_barrier(jnp.sum(kernel * source[:, 4, None, :], axis=2)), None)
        nearby, _ = lax.scan(near_step, jnp.zeros((group, panels), jnp.float32), near_block.T)
        gathered = poles[far_block]
        segment_keys = (jnp.arange(group, dtype=jnp.int32)[:, None] * offsets + offset_block).reshape(-1)
        summed = jax.ops.segment_sum(gathered.reshape(-1, terms), segment_keys, num_segments=group * offsets)
        local = jnp.einsum('tok,oik->ti', summed.reshape(group, offsets, terms), table, precision=highest)
        return (nearby, local)
    nearby, local = lax.map(segment_work, (coords.reshape(-1, group, 3, panels), near_rows.reshape(-1, group, near_list.shape[1]), far_rows.reshape(-1, group, far_count), far_offset.reshape(-1, group, far_count)))
    nearby = nearby.reshape(leaves, panels)
    local = local.reshape(leaves, terms).astype(jnp.bfloat16)
    local = lax.optimization_barrier(local)
    distant = jnp.einsum('lpk,lk->lp', l2p.astype(jnp.float32), local.astype(jnp.float32), precision=highest)
    image = (0.5 * current + nearby + distant) * live_mask
    masked = basis * live_mask[None]
    population = jnp.sum(live_mask) * panels
    coefficients = jnp.einsum('jlp,lp->j', masked, image, precision=highest) / population
    residue = image - jnp.einsum('j,jlp->lp', coefficients, masked, precision=highest)
    scale = jnp.sqrt(jnp.sum(residue * residue) / population + epsilon)
    return (residue / scale, jnp.concatenate([coefficients, scale[None]]))
```

```python
import functools

import jax
import jax.numpy as jnp
from jax import lax
from jax.experimental import pallas as pl
from jax.experimental.pallas import tpu as pltpu
from jax.sharding import PartitionSpec as P

four_pi = 12.566370614359172
epsilon = 1e-06
bf16 = jnp.bfloat16
f32 = jnp.float32
WIDTH = 32
LIMIT = 56 * 1024 * 1024

across = (((1,), (1,)), ((), ()))


def vmem(count):
    return [pl.BlockSpec(memory_space=pltpu.VMEM)] * count


def smem(count):
    return [pl.BlockSpec(memory_space=pltpu.SMEM)] * count


def live_rows(counts, shape):
    return (lax.broadcasted_iota(jnp.int32, shape, 0) < counts[0]).astype(f32)


def prep_kernel(counts, basis, coords, areas, p2m, block):
    krylov, leaves, panels = basis.shape
    terms = p2m.shape[1]
    current = basis[krylov - 1] * live_rows(counts, (leaves, panels))
    rounded = current.astype(bf16)
    row = lax.broadcasted_iota(jnp.int32, (leaves, terms), 0)
    poles = jnp.zeros((leaves, terms), f32)
    for leaf in range(leaves):
        moved = lax.dot_general(rounded, p2m[leaf], across, preferred_element_type=f32)
        poles = jnp.where(row == leaf, moved, poles)
    for c in range(3):
        block[c] = coords[:, c, :]
    block[3] = areas[...]
    block[4] = areas[...] * current * (1.0 / four_pi)
    block[5] = jnp.zeros((leaves, panels), f32)
    block[5, :, 0:terms] = poles


def plan_kernel(counts, basis, slots, classes, hits, gram, wide):
    krylov, leaves, panels = basis.shape
    total = hits.shape[0] // leaves
    window = hits.shape[1]
    panes = wide.shape[0]
    lanes = wide.shape[2]
    entries = slots.shape[1]

    def body(leaf, carry):
        offset = classes[pl.ds(leaf, 1), :]
        slot = slots[pl.ds(leaf, 1), :]
        by_class = lax.broadcasted_iota(jnp.int32, (total, entries), 0) == offset
        by_slot = lax.broadcasted_iota(jnp.int32, (window, entries), 0) == slot
        found = lax.dot_general(
            by_class.astype(f32).astype(bf16),
            by_slot.astype(f32).astype(bf16),
            across,
            preferred_element_type=f32,
        )
        for pane in range(panes):
            part = found[:, pane * lanes : (pane + 1) * lanes]
            wide[pane, pl.ds(leaf, total, stride=leaves), :] = part
        return carry

    lax.fori_loop(0, leaves, body, 0)

    rows = 16 * leaves

    def shrink(step, carry):
        at = pl.ds(pl.multiple_of(step * rows, rows), rows)
        for pane in range(panes):
            hits[at, pane * lanes : (pane + 1) * lanes] = wide[pane, at, :].astype(bf16)
        return carry

    lax.fori_loop(0, hits.shape[0] // rows, shrink, 0)

    live = live_rows(counts, (leaves, panels))
    masked = [basis[j] * live for j in range(krylov)]
    lane = lax.broadcasted_iota(jnp.int32, (krylov, panels), 1)
    tile = jnp.zeros((krylov, panels), f32)
    for j in range(krylov):
        rows_j = [jnp.sum(masked[i] * masked[j], axis=0, keepdims=True) for i in range(krylov)]
        column = jnp.sum(jnp.concatenate(rows_j, axis=0), axis=1, keepdims=True)
        tile = jnp.where(lane == krylov + j, column, tile)
    population = (jnp.minimum(counts[0], leaves) * panels).astype(f32)
    gram[...] = jnp.where(lane == 2, population, tile)


def thirds(value):
    first = value.astype(bf16).astype(f32)
    second = (value - first).astype(bf16).astype(f32)
    return first, second, value - first - second


pairs = ((0, 0), (0, 1), (1, 0), (1, 1), (0, 2), (2, 0))


def main_kernel(
    counts, near, here, there, hits_hbm, m2l_hbm, l2p, basis, gram,
    image_out, tile_out,
    hits, m2l, source32, source16, target32, charge, poles32, poles16, nearby, sems,
):
    krylov, leaves, panels = basis.shape
    blocks = here.shape[0]
    terms = l2p.shape[2]
    offsets = m2l.shape[0]
    copies = [
        pltpu.make_async_copy(hits_hbm, hits, sems.at[0]),
        pltpu.make_async_copy(m2l_hbm, m2l, sems.at[1]),
    ]
    for copy in copies:
        copy.start()

    ones = jnp.ones((leaves, panels), f32)
    zeros = jnp.zeros((leaves, panels), f32)

    def place(ref, base, rows):
        for k in range(WIDTH):
            value = rows[k] if k < len(rows) else zeros
            ref[pl.ds(base * WIDTH + k, leaves, stride=WIDTH), :] = value

    poles32[...] = jnp.zeros_like(poles32)
    for b in range(2 * blocks):
        got = here if b < blocks else there
        at = b % blocks
        point = [got[at, c] for c in range(3)]
        area = got[at, 3]
        area = jnp.where(area > 0.0, area, 1.0)
        split = [thirds(p) for p in point]
        square = point[0] * point[0] + point[1] * point[1] + point[2] * point[2]
        rows = [split[c][q] for c in range(3) for (_, q) in pairs]
        place(source32, b * leaves, rows + list(thirds(square + area)) + [ones] * 3)
        if b == 0:
            rows = [split[c][p] * (-2.0) for c in range(3) for (p, _) in pairs]
            place(target32, 0, rows + [ones] * 3 + list(thirds(square)))
        charge[pl.ds(b * leaves, leaves), :] = got[at, 4]
        poles32[pl.ds(b * leaves, leaves), :] = got[at, 5]
    source16[...] = source32[...].astype(bf16)
    pole = poles32[...]
    pole_high = pole.astype(bf16)
    poles16[:, 0:panels] = pole_high
    poles16[:, panels : 2 * panels] = (pole - pole_high.astype(f32)).astype(bf16)

    entries = near.shape[1]
    row_ones = jnp.ones((8, panels), f32)

    def near_body(leaf, carry):
        at = pl.multiple_of(leaf * WIDTH, WIDTH)
        target = target32[pl.ds(at, WIDTH), :].T.astype(bf16)
        total = jnp.zeros((panels, panels), f32)
        for start in range(0, entries, 2):
            ids = [near[leaf, e] for e in range(start, min(start + 2, entries))]
            source = [source16[pl.ds(pl.multiple_of(s * WIDTH, WIDTH), WIDTH), :] for s in ids]
            source = jnp.concatenate(source, axis=1) if len(ids) > 1 else source[0]
            inverse = lax.rsqrt(jnp.dot(target, source, preferred_element_type=f32))
            for e, s in enumerate(ids):
                total += inverse[:, e * panels : (e + 1) * panels] * charge[pl.ds(s, 1), :]
        summed = lax.dot_general(
            row_ones, total, across, preferred_element_type=f32, precision=lax.Precision.HIGHEST
        )
        nearby[pl.ds(leaf, 1), :] = summed[0:1]
        return carry

    lax.fori_loop(0, leaves, near_body, 0)
    for copy in copies:
        copy.wait()

    chunk = 16
    steps = hits.shape[0] // leaves // chunk

    def far_body(step, local):
        at = pl.multiple_of(step * chunk * leaves, chunk * leaves)
        both = jnp.dot(
            hits[pl.ds(at, chunk * leaves), :], poles16[...], preferred_element_type=f32
        )
        summed = both[:, 0:panels] + both[:, panels : 2 * panels]
        for i in range(chunk):
            part = summed[i * leaves : (i + 1) * leaves, 0:terms]
            high = part.astype(bf16).astype(f32)
            stacked = jnp.concatenate([high, part - high], axis=0).astype(bf16)
            table = m2l[jnp.minimum(step * chunk + i, offsets - 1)]
            local += lax.dot_general(stacked, table, across, preferred_element_type=f32)
        return local

    local = lax.fori_loop(0, steps, far_body, jnp.zeros((2 * leaves, terms), f32))
    local16 = (local[0:leaves] + local[leaves:]).astype(bf16)
    row = lax.broadcasted_iota(jnp.int32, (leaves, panels), 0)
    distant = jnp.zeros((leaves, panels), f32)
    for leaf in range(leaves):
        moved = lax.dot_general(local16, l2p[leaf], across, preferred_element_type=f32)
        distant = jnp.where(row == leaf, moved, distant)

    live = live_rows(counts, (leaves, panels))
    current = basis[krylov - 1] * live
    image = (0.5 * current + nearby[...] + distant) * live
    image_out[...] = image
    rows = [jnp.sum(basis[j] * live * image, axis=0, keepdims=True) for j in range(krylov)]
    product = jnp.sum(jnp.concatenate(rows, axis=0), axis=1, keepdims=True)
    energy = jnp.sum(jnp.sum(image * image, axis=0, keepdims=True), axis=1, keepdims=True)
    lane = lax.broadcasted_iota(jnp.int32, (krylov, panels), 1)
    tile_out[...] = jnp.where(lane == 0, product, jnp.where(lane == 1, energy, gram[...]))


def final_kernel(counts, basis, image, tile, vector, column):
    krylov, leaves, panels = basis.shape
    sums = tile[...]
    population = sums[0:1, 2:3]
    energy = sums[0:1, 1:2]
    products = sums[:, 0:1]
    coefficients = products / population
    row = lax.broadcasted_iota(jnp.int32, (krylov, panels), 0)
    lane = lax.broadcasted_iota(jnp.int32, (krylov, panels), 1)
    in_gram = (lane >= krylov) & (lane < 2 * krylov)
    applied = jnp.sum(jnp.where(in_gram, coefficients * sums, 0.0), axis=0, keepdims=True)
    across_lanes = jnp.sum(jnp.where(lane == krylov + row, coefficients, 0.0), axis=0, keepdims=True)
    curvature = jnp.sum(applied * across_lanes, axis=1, keepdims=True)
    crossed = jnp.sum(coefficients * products, axis=0, keepdims=True)
    squares = energy - 2.0 * crossed + curvature
    scale = jnp.sqrt(squares / population + epsilon)
    live = live_rows(counts, (leaves, panels))
    residue = image[...]
    for j in range(krylov):
        residue = residue - coefficients[j : j + 1, 0:1] * (basis[j] * live)
    vector[...] = residue / scale
    placed = jnp.sum(jnp.where(lane == row, coefficients, 0.0), axis=0, keepdims=True)
    column[...] = jnp.where(lane[0:1] == krylov, scale, placed)


def swap(value, axis, bit):
    count = lax.axis_size(axis)
    return lax.ppermute(value, axis, [(i, i ^ bit) for i in range(count)])


def hop(value, axis):
    count = lax.axis_size(axis)
    moves = [(i, i + 2 if i % 2 == 0 else i - 2) for i in range(count)]
    return lax.ppermute(value, axis, [(i, k) for i, k in moves if 0 <= k < count])


def on_device(basis, coords, areas, p2m, l2p, m2l, counts, near_list, far_list, far_offset):
    krylov, leaves, panels = basis.shape
    terms = p2m.shape[1]
    offsets = m2l.shape[0]
    groups = lax.axis_size("grp")
    params = pltpu.CompilerParams(vmem_limit_bytes=LIMIT)
    me = lax.axis_index("grp")
    even = lax.axis_index("seg") % 2 == 0

    block = pl.pallas_call(
        prep_kernel,
        out_shape=jax.ShapeDtypeStruct((6, leaves, panels), f32),
        in_specs=smem(1) + vmem(4),
        out_specs=pl.BlockSpec(memory_space=pltpu.VMEM),
        compiler_params=params,
        name="prep",
    )(counts, basis, coords, areas, p2m)

    half = groups // 2

    def slot_of(window):
        segment = window // (groups * leaves)
        group = (window // leaves) % groups
        order = jnp.where(segment == 1, 0, jnp.where((segment == 2) == even, 1, 2))
        relative = group ^ me
        return ((relative % 2) * 3 * half + order * half + relative // 2) * leaves + window % leaves

    near_slots = slot_of(near_list)
    pad = -far_list.shape[1] % 128
    slots = jnp.pad(slot_of(far_list), ((0, 0), (0, pad)), constant_values=-1)
    classes = jnp.pad(far_offset, ((0, 0), (0, pad)), constant_values=-1)
    window = 3 * groups * leaves
    wide = window + -window % 128
    total = offsets + -offsets % 16
    hits, gram = pl.pallas_call(
        plan_kernel,
        out_shape=(
            jax.ShapeDtypeStruct((total * leaves, wide), bf16),
            jax.ShapeDtypeStruct((krylov, panels), f32),
        ),
        in_specs=smem(1) + vmem(3),
        out_specs=tuple(vmem(2)),
        scratch_shapes=[pltpu.VMEM((wide // 128, total * leaves, 128), f32)],
        compiler_params=params,
        name="plan",
    )(counts, basis, slots, classes)

    def spread(value):
        whole = [value]
        bit = 2
        while bit < groups:
            whole = whole + [swap(v, "grp", bit) for v in whole]
            bit *= 2
        return whole

    beside = swap(block, "seg", 1)
    own = spread(block)
    beyond = hop(beside, "seg")
    here = jnp.stack(own + spread(beside) + spread(beyond))
    there = swap(here, "grp", 1)

    image, tile = pl.pallas_call(
        main_kernel,
        out_shape=(
            jax.ShapeDtypeStruct((leaves, panels), f32),
            jax.ShapeDtypeStruct((krylov, panels), f32),
        ),
        in_specs=smem(2) + vmem(2) + [pl.BlockSpec(memory_space=pl.ANY)] * 2 + vmem(3),
        out_specs=tuple(vmem(2)),
        scratch_shapes=[
            pltpu.VMEM((total * leaves, wide), bf16),
            pltpu.VMEM(m2l.shape, bf16),
            pltpu.VMEM((window * WIDTH, panels), f32),
            pltpu.VMEM((window * WIDTH, panels), bf16),
            pltpu.VMEM((leaves * WIDTH, panels), f32),
            pltpu.VMEM((window, panels), f32),
            pltpu.VMEM((wide, panels), f32),
            pltpu.VMEM((wide, 2 * panels), bf16),
            pltpu.VMEM((leaves, panels), f32),
            pltpu.SemaphoreType.DMA((2,)),
        ],
        compiler_params=params,
        name="main",
    )(counts, near_slots, here, there, hits, m2l, l2p, basis, gram)

    for axis in ("grp", "seg"):
        bit = 1
        while bit < lax.axis_size(axis):
            tile = tile + swap(tile, axis, bit)
            bit *= 2

    vector, column = pl.pallas_call(
        final_kernel,
        out_shape=(
            jax.ShapeDtypeStruct((leaves, panels), f32),
            jax.ShapeDtypeStruct((1, panels), f32),
        ),
        in_specs=smem(1) + vmem(3),
        out_specs=tuple(vmem(2)),
        compiler_params=params,
        name="final",
    )(counts, basis, image, tile)
    return vector, column[0, : krylov + 1]


def solution(mesh):
    placed = (
        P(None, ("seg", "grp"), None),
        P(("seg", "grp"), None, None),
        P(("seg", "grp"), None),
        P(("seg", "grp"), None, None),
        P(("seg", "grp"), None, None),
        P(),
        P(("seg", "grp")),
        P(("seg", "grp"), None),
        P(("seg", "grp"), None),
        P(("seg", "grp"), None),
    )
    return jax.shard_map(
        on_device,
        mesh=mesh,
        in_specs=placed,
        out_specs=(P(("seg", "grp"), None), P()),
        check_vma=False,
    )
```

```python
import functools

import jax
import jax.numpy as jnp
from jax import lax
from jax.experimental import pallas as pl
from jax.experimental.pallas import tpu as pltpu
from jax.sharding import PartitionSpec as P

four_pi = 12.566370614359172
epsilon = 1e-06
bf16 = jnp.bfloat16
f32 = jnp.float32
WIDTH = 32
LIMIT = 56 * 1024 * 1024

across = (((1,), (1,)), ((), ()))


def vmem(count):
    return [pl.BlockSpec(memory_space=pltpu.VMEM)] * count


def smem(count):
    return [pl.BlockSpec(memory_space=pltpu.SMEM)] * count


def live_rows(counts, shape):
    return (lax.broadcasted_iota(jnp.int32, shape, 0) < counts[0]).astype(f32)


def prep_kernel(counts, basis, coords, areas, p2m, block):
    leaves, panels = areas.shape
    terms = p2m.shape[0]
    current = basis[basis.shape[0] - 1] * live_rows(counts, (leaves, panels))
    rounded = current.astype(bf16).astype(f32)
    lane = lax.broadcasted_iota(jnp.int32, (leaves, panels), 1)
    poles = jnp.zeros((leaves, panels), f32)
    for k in range(terms):
        moved = jnp.sum(p2m[k].astype(f32) * rounded, axis=1, keepdims=True)
        poles = jnp.where(lane == k, moved, poles)
    for c in range(3):
        block[c] = coords[c]
    block[3] = areas[...]
    block[4] = areas[...] * current * (1.0 / four_pi)
    block[5] = poles


def plan_kernel(groups, counts, place, basis, near, far, offset, near_slots, slots, classes, gram):
    krylov, leaves, panels = basis.shape
    half = groups // 2
    span = groups * leaves
    me = place[0]
    order_low = place[1]

    def slot_of(window):
        low = (window < span).astype(jnp.int32)
        high = (window >= 2 * span).astype(jnp.int32)
        order = low * order_low + high * (3 - order_low)
        inner = window - span * (1 - low + high)
        group = jnp.zeros_like(window)
        for g in range(1, groups):
            group += (inner >= g * leaves).astype(jnp.int32)
        relative = group ^ me
        core = relative & 1
        column = core * (3 * half) + order * half + lax.shift_right_logical(relative, 1)
        return column * leaves + inner - group * leaves

    near_slots[...] = slot_of(near[...])
    count = far.shape[1]
    slots[...] = jnp.full(slots.shape, -1, jnp.int32)
    slots[:, 0:count] = slot_of(far[...])
    classes[...] = jnp.full(classes.shape, -1, jnp.int32)
    classes[:, 0:count] = offset[...]

    live = live_rows(counts, (leaves, panels))
    masked = [basis[j] * live for j in range(krylov)]
    lane = lax.broadcasted_iota(jnp.int32, (krylov, panels), 1)
    tile = jnp.zeros((krylov, panels), f32)
    for j in range(krylov):
        rows_j = [jnp.sum(masked[i] * masked[j], axis=0, keepdims=True) for i in range(krylov)]
        column = jnp.sum(jnp.concatenate(rows_j, axis=0), axis=1, keepdims=True)
        tile = jnp.where(lane == krylov + j, column, tile)
    population = (jnp.minimum(counts[0], leaves) * panels).astype(f32)
    gram[...] = jnp.where(lane == 2, population, tile)


def thirds(value):
    first = value.astype(bf16).astype(f32)
    second = (value - first).astype(bf16).astype(f32)
    return first, second, value - first - second


pairs = ((0, 0), (0, 1), (1, 0), (1, 1), (0, 2), (2, 0))


def main_kernel(
    counts, near, here, there, slots, classes, m2l_hbm, l2p, basis, gram,
    image_out, tile_out,
    m2l, source32, source16, target32, target16, charge, poles32, sums, totals, found, sem,
):
    krylov, leaves, panels = basis.shape
    blocks = here.shape[0]
    terms = l2p.shape[0]
    offsets = m2l.shape[1]
    padded = found.shape[1]
    entries = slots.shape[1]
    copy = pltpu.make_async_copy(m2l_hbm, m2l, sem)
    copy.start()

    ones = jnp.ones((leaves, panels), f32)
    zeros = jnp.zeros((leaves, panels), f32)

    def place(ref, base, rows):
        for k in range(WIDTH):
            value = rows[k] if k < len(rows) else zeros
            ref[pl.ds(base * WIDTH + k, leaves, stride=WIDTH), :] = value

    poles32[...] = jnp.zeros_like(poles32)
    for b in range(2 * blocks):
        got = here if b < blocks else there
        at = b % blocks
        point = [got[at, c] for c in range(3)]
        area = got[at, 3]
        area = jnp.where(area > 0.0, area, 1.0)
        split = [thirds(p) for p in point]
        square = point[0] * point[0] + point[1] * point[1] + point[2] * point[2]
        rows = [split[c][q] for c in range(3) for (_, q) in pairs]
        place(source32, b * leaves, rows + list(thirds(square + area)) + [ones] * 3)
        if b == 0:
            rows = [split[c][p] * (-2.0) for c in range(3) for (p, _) in pairs]
            place(target32, 0, rows + [ones] * 3 + list(thirds(square)))
        charge[pl.ds(b * leaves, leaves), :] = got[at, 4]
        poles32[pl.ds(b * leaves, leaves), :] = got[at, 5]
    source16[...] = source32[...].astype(bf16)
    for leaf in range(leaves):
        target16[leaf] = target32[leaf * WIDTH : (leaf + 1) * WIDTH, :].T.astype(bf16)

    neighbours = near.shape[1]

    def near_body(leaf):
        total = jnp.zeros((panels, panels), f32)
        for start in range(0, neighbours, 2):
            ids = [near[leaf, e] for e in range(start, min(start + 2, neighbours))]
            source = [source16[pl.ds(pl.multiple_of(s * WIDTH, WIDTH), WIDTH), :] for s in ids]
            source = jnp.concatenate(source, axis=1) if len(ids) > 1 else source[0]
            inverse = lax.rsqrt(jnp.dot(target16[leaf], source, preferred_element_type=f32))
            for e, s in enumerate(ids):
                total += inverse[:, e * panels : (e + 1) * panels] * charge[pl.ds(s, 1), :]
        totals[leaf] = total

    repeat(leaves, 4, near_body)
    nearby = jnp.concatenate(
        [jnp.sum(totals[leaf].T, axis=0, keepdims=True) for leaf in range(leaves)], axis=0
    )

    pole = poles32[...].T
    high = pole.astype(bf16)
    poles16 = jnp.concatenate([high, (pole - high.astype(f32)).astype(bf16)], axis=0)
    window = poles16.shape[1]

    def class_body(leaf):
        slot = slots[pl.ds(leaf, 1), :]
        offset = classes[pl.ds(leaf, 1), :]
        by_slot = lax.broadcasted_iota(jnp.int32, (window, entries), 0) == slot
        by_class = lax.broadcasted_iota(jnp.int32, (padded, entries), 0) == offset
        taken = jnp.dot(poles16, by_slot.astype(f32).astype(bf16), preferred_element_type=f32)
        both = lax.dot_general(
            by_class.astype(f32).astype(bf16),
            taken.astype(bf16),
            across,
            preferred_element_type=f32,
        )
        found[leaf] = both[:, 0:panels] + both[:, panels : 2 * panels]

    repeat(leaves, 4, class_body)
    copy.wait()

    group = 8
    filler = jnp.zeros((terms * group, panels - terms), bf16)

    def translate(table, at):
        part = found[:, pl.ds(at, group), :].reshape(leaves * group, panels)
        first = part.astype(bf16)
        second = (part - first.astype(f32)).astype(bf16)
        table = jnp.concatenate([table.reshape(terms * group, terms), filler], axis=1)
        return lax.dot_general(
            jnp.concatenate([table, table], axis=1),
            jnp.concatenate([first, second], axis=1),
            across,
            preferred_element_type=f32,
        )

    full = offsets // group
    rest = offsets % group
    sums[...] = jnp.zeros_like(sums)
    if rest:
        tail = m2l[:, full * group : offsets, :].astype(f32)
        tail = jnp.concatenate([tail, jnp.zeros((terms, group - rest, terms), f32)], axis=1)
        sums[...] = translate(tail.reshape(terms * group, terms).astype(bf16), full * group)
    batch = next(n for n in range(min(13, full), 0, -1) if full % n == 0)

    def far_body(step, carry):
        value = None
        for i in range(batch):
            at = pl.multiple_of((step * batch + i) * group, group)
            one = translate(m2l[:, pl.ds(at, group), :], at)
            value = one if value is None else value + one
        sums[...] += value
        return carry

    lax.fori_loop(0, full // batch, far_body, 0)
    spread = leaves * group
    row = lax.broadcasted_iota(jnp.int32, (terms * group, spread), 0) & (group - 1)
    lane = lax.broadcasted_iota(jnp.int32, (terms * group, spread), 1) & (group - 1)
    kept = jnp.where(row == lane, sums[...], 0.0)
    kept = jnp.sum(kept.reshape(terms, group, spread), axis=1)
    owner = lax.broadcasted_iota(jnp.int32, (leaves, spread), 0) * group
    lane = lax.broadcasted_iota(jnp.int32, (leaves, spread), 1)
    pick = ((lane >= owner) & (lane < owner + group)).astype(f32).astype(bf16)
    local = jnp.zeros((leaves, terms), f32)
    for part in thirds(kept):
        local += lax.dot_general(pick, part.astype(bf16), across, preferred_element_type=f32)
    local = local.astype(bf16).astype(f32)
    distant = zeros
    for k in range(terms):
        distant += l2p[k].astype(f32) * local[:, k : k + 1]

    live = live_rows(counts, (leaves, panels))
    current = basis[krylov - 1] * live
    image = (0.5 * current + nearby + distant) * live
    image_out[...] = image
    rows = [jnp.sum(basis[j] * live * image, axis=0, keepdims=True) for j in range(krylov)]
    product = jnp.sum(jnp.concatenate(rows, axis=0), axis=1, keepdims=True)
    energy = jnp.sum(jnp.sum(image * image, axis=0, keepdims=True), axis=1, keepdims=True)
    lane = lax.broadcasted_iota(jnp.int32, (krylov, panels), 1)
    tile_out[...] = jnp.where(lane == 0, product, jnp.where(lane == 1, energy, gram[...]))


def repeat(count, most, body):
    batch = next(n for n in range(most, 0, -1) if count % n == 0)

    def several(step, carry):
        for i in range(batch):
            body(step * batch + i)
        return carry

    lax.fori_loop(0, count // batch, several, 0)


def final_kernel(counts, basis, image, tile, vector, column):
    krylov, leaves, panels = basis.shape
    sums = tile[...]
    population = sums[0:1, 2:3]
    energy = sums[0:1, 1:2]
    products = sums[:, 0:1]
    coefficients = products / population
    row = lax.broadcasted_iota(jnp.int32, (krylov, panels), 0)
    lane = lax.broadcasted_iota(jnp.int32, (krylov, panels), 1)
    in_gram = (lane >= krylov) & (lane < 2 * krylov)
    applied = jnp.sum(jnp.where(in_gram, coefficients * sums, 0.0), axis=0, keepdims=True)
    across_lanes = jnp.sum(jnp.where(lane == krylov + row, coefficients, 0.0), axis=0, keepdims=True)
    curvature = jnp.sum(applied * across_lanes, axis=1, keepdims=True)
    crossed = jnp.sum(coefficients * products, axis=0, keepdims=True)
    squares = energy - 2.0 * crossed + curvature
    scale = jnp.sqrt(squares / population + epsilon)
    live = live_rows(counts, (leaves, panels))
    residue = image[...]
    for j in range(krylov):
        residue = residue - coefficients[j : j + 1, 0:1] * (basis[j] * live)
    vector[...] = residue / scale
    placed = jnp.sum(jnp.where(lane == row, coefficients, 0.0), axis=0, keepdims=True)
    column[...] = jnp.where(lane[0:1] == krylov, scale, placed)


def swap(value, axis, bit):
    count = lax.axis_size(axis)
    return lax.ppermute(value, axis, [(i, i ^ bit) for i in range(count)])


def hop(value, axis):
    count = lax.axis_size(axis)
    moves = [(i, i + 2 if i % 2 == 0 else i - 2) for i in range(count)]
    return lax.ppermute(value, axis, [(i, k) for i, k in moves if 0 <= k < count])


def on_device(basis, coords, areas, p2m, l2p, m2l, counts, near_list, far_list, far_offset):
    krylov, leaves, panels = basis.shape
    coords = jnp.transpose(coords, (1, 0, 2))
    p2m = jnp.transpose(p2m, (1, 0, 2))
    l2p = jnp.transpose(l2p, (2, 0, 1))
    m2l = jnp.transpose(m2l, (1, 0, 2))
    terms, offsets = m2l.shape[:2]
    groups = lax.axis_size("grp")
    params = pltpu.CompilerParams(vmem_limit_bytes=LIMIT)
    even = 1 - lax.axis_index("seg") % 2
    position = jnp.stack([lax.axis_index("grp"), 1 + even]).astype(jnp.int32)

    block = pl.pallas_call(
        prep_kernel,
        out_shape=jax.ShapeDtypeStruct((6, leaves, panels), f32),
        in_specs=smem(1) + vmem(4),
        out_specs=pl.BlockSpec(memory_space=pltpu.VMEM),
        compiler_params=params,
        name="prep",
    )(counts, basis, coords, areas, p2m)

    window = 3 * groups * leaves
    wide = window + -window % 128
    entries = far_list.shape[1] + -far_list.shape[1] % 128
    padded = offsets + -offsets % 16
    near_slots, slots, classes, gram = pl.pallas_call(
        functools.partial(plan_kernel, groups),
        out_shape=(
            jax.ShapeDtypeStruct(near_list.shape, jnp.int32),
            jax.ShapeDtypeStruct((leaves, entries), jnp.int32),
            jax.ShapeDtypeStruct((leaves, entries), jnp.int32),
            jax.ShapeDtypeStruct((krylov, panels), f32),
        ),
        in_specs=smem(2) + vmem(4),
        out_specs=tuple(vmem(4)),
        compiler_params=params,
        name="plan",
    )(counts, position, basis, near_list, far_list, far_offset)

    def spread(value):
        whole = [value]
        bit = 2
        while bit < groups:
            whole = whole + [swap(v, "grp", bit) for v in whole]
            bit *= 2
        return whole

    beside = swap(block, "seg", 1)
    own = spread(block)
    beyond = hop(beside, "seg")
    here = jnp.stack(own + spread(beside) + spread(beyond))
    there = swap(here, "grp", 1)

    image, tile = pl.pallas_call(
        main_kernel,
        out_shape=(
            jax.ShapeDtypeStruct((leaves, panels), f32),
            jax.ShapeDtypeStruct((krylov, panels), f32),
        ),
        in_specs=smem(2) + vmem(4) + [pl.BlockSpec(memory_space=pl.ANY)] + vmem(3),
        out_specs=tuple(vmem(2)),
        scratch_shapes=[
            pltpu.VMEM(m2l.shape, bf16),
            pltpu.VMEM((window * WIDTH, panels), f32),
            pltpu.VMEM((window * WIDTH, panels), bf16),
            pltpu.VMEM((leaves * WIDTH, panels), f32),
            pltpu.VMEM((leaves, panels, WIDTH), bf16),
            pltpu.VMEM((window, panels), f32),
            pltpu.VMEM((wide, panels), f32),
            pltpu.VMEM((terms * 8, leaves * 8), f32),
            pltpu.VMEM((leaves, panels, panels), f32),
            pltpu.VMEM((leaves, padded, panels), f32),
            pltpu.SemaphoreType.DMA,
        ],
        compiler_params=params,
        name="main",
    )(counts, near_slots, here, there, slots, classes, m2l, l2p, basis, gram)

    for axis in ("grp", "seg"):
        bit = 1
        while bit < lax.axis_size(axis):
            tile = tile + swap(tile, axis, bit)
            bit *= 2

    vector, column = pl.pallas_call(
        final_kernel,
        out_shape=(
            jax.ShapeDtypeStruct((leaves, panels), f32),
            jax.ShapeDtypeStruct((1, panels), f32),
        ),
        in_specs=smem(1) + vmem(3),
        out_specs=tuple(vmem(2)),
        compiler_params=params,
        name="final",
    )(counts, basis, image, tile)
    return vector, column[0, : krylov + 1]


def solution(mesh):
    placed = (
        P(None, ("seg", "grp"), None),
        P(("seg", "grp"), None, None),
        P(("seg", "grp"), None),
        P(("seg", "grp"), None, None),
        P(("seg", "grp"), None, None),
        P(),
        P(("seg", "grp")),
        P(("seg", "grp"), None),
        P(("seg", "grp"), None),
        P(("seg", "grp"), None),
    )
    return jax.shard_map(
        on_device,
        mesh=mesh,
        in_specs=placed,
        out_specs=(P(("seg", "grp"), None), P()),
        check_vma=False,
    )
```

```python
import functools

import jax
import jax.numpy as jnp
from jax import lax
from jax.experimental import pallas as pl
from jax.experimental.pallas import tpu as pltpu
from jax.sharding import PartitionSpec as P

four_pi = 12.566370614359172
epsilon = 1e-06
bf16 = jnp.bfloat16
f32 = jnp.float32
WIDTH = 16
CENTRE = 2.0
LIMIT = 56 * 1024 * 1024

across = (((1,), (1,)), ((), ()))


def vmem(count):
    return [pl.BlockSpec(memory_space=pltpu.VMEM)] * count


def smem(count):
    return [pl.BlockSpec(memory_space=pltpu.SMEM)] * count


def live_rows(counts, shape):
    return (lax.broadcasted_iota(jnp.int32, shape, 0) < counts[0]).astype(f32)


def prep_kernel(counts, basis, coords, areas, p2m, block):
    leaves, panels = areas.shape
    terms = p2m.shape[0]
    current = basis[basis.shape[0] - 1] * live_rows(counts, (leaves, panels))
    rounded = current.astype(bf16).astype(f32)
    lane = lax.broadcasted_iota(jnp.int32, (leaves, panels), 1)
    poles = jnp.zeros((leaves, panels), f32)
    for k in range(terms):
        moved = jnp.sum(p2m[k].astype(f32) * rounded, axis=1, keepdims=True)
        poles = jnp.where(lane == k, moved, poles)
    for c in range(3):
        block[c] = coords[c]
    block[3] = areas[...]
    block[4] = areas[...] * current * (1.0 / four_pi)
    block[5] = poles


def slot_of(window, groups, leaves, me, order_low):
    half = groups // 2
    span = groups * leaves
    low = (window < span).astype(jnp.int32)
    high = (window >= 2 * span).astype(jnp.int32)
    order = low * order_low + high * (3 - order_low)
    inner = window - span * (1 - low + high)
    group = jnp.zeros_like(window)
    for g in range(1, groups):
        group += (inner >= g * leaves).astype(jnp.int32)
    relative = group ^ me
    column = (relative & 1) * (3 * half) + order * half + lax.shift_right_logical(relative, 1)
    return column * leaves + inner - group * leaves


def tally_kernel(groups, leaves, first, after, place, far, offset, hits, slots, classes):
    held, padded, wide = hits.shape
    count = far.shape[1]
    entries = slots.shape[1]
    rows = pl.ds(first, held)
    slots[...] = jnp.full(slots.shape, -1, jnp.int32)
    slots[:, 0:count] = slot_of(far[rows, :], groups, leaves, place[0], place[1])
    classes[...] = jnp.full(classes.shape, -1, jnp.int32)
    classes[:, 0:count] = offset[rows, :]

    def body(leaf):
        slot = slots[pl.ds(leaf, 1), :]
        of_class = classes[pl.ds(leaf, 1), :]
        by_slot = lax.broadcasted_iota(jnp.int32, (wide, entries), 0) == slot
        by_class = lax.broadcasted_iota(jnp.int32, (padded, entries), 0) == of_class
        hits[leaf] = lax.dot_general(
            by_class.astype(f32).astype(bf16),
            by_slot.astype(f32).astype(bf16),
            across,
            preferred_element_type=f32,
        ).astype(bf16)

    repeat(held, 4, body)


def plan_kernel(groups, counts, place, basis, near, near_slots, gram):
    krylov, leaves, panels = basis.shape
    near_slots[...] = slot_of(near[...], groups, leaves, place[0], place[1])
    live = live_rows(counts, (leaves, panels))
    masked = [basis[j] * live for j in range(krylov)]
    lane = lax.broadcasted_iota(jnp.int32, (krylov, panels), 1)
    tile = jnp.zeros((krylov, panels), f32)
    for j in range(krylov):
        rows_j = [jnp.sum(masked[i] * masked[j], axis=0, keepdims=True) for i in range(krylov)]
        column = jnp.sum(jnp.concatenate(rows_j, axis=0), axis=1, keepdims=True)
        tile = jnp.where(lane == krylov + j, column, tile)
    population = (jnp.minimum(counts[0], leaves) * panels).astype(f32)
    gram[...] = jnp.where(lane == 2, population, tile)


def thirds(value):
    first = value.astype(bf16).astype(f32)
    second = (value - first).astype(bf16).astype(f32)
    return first, second, value - first - second


pairs = ((0, 0), (0, 1), (1, 0))


def main_kernel(pieces, tallies, *refs):
    counts, near = refs[0:2]
    blocks = refs[2 : 2 + pieces]
    hits_hbm = refs[2 + pieces : 2 + pieces + tallies]
    m2l_hbm, l2p, basis, gram, image_out, tile_out = refs[2 + pieces + tallies : 8 + pieces + tallies]
    hits, m2l, source32, source16, target32, target16 = refs[8 + pieces + tallies : 14 + pieces + tallies]
    charge, poles32, sums, totals, found, sems = refs[14 + pieces + tallies :]
    krylov, leaves, panels = basis.shape
    terms = l2p.shape[0]
    offsets = m2l.shape[1]
    held = leaves // tallies
    copies = [
        pltpu.make_async_copy(hits_hbm[i], hits.at[pl.ds(i * held, held)], sems.at[i])
        for i in range(tallies)
    ]
    copies.append(pltpu.make_async_copy(m2l_hbm, m2l, sems.at[tallies]))
    for copy in copies:
        copy.start()

    ones = jnp.ones((leaves, panels), f32)
    zeros = jnp.zeros((leaves, panels), f32)

    def place(ref, base, rows):
        for k in range(WIDTH):
            value = rows[k] if k < len(rows) else zeros
            ref[pl.ds(base * WIDTH + k, leaves, stride=WIDTH), :] = value

    poles32[...] = jnp.zeros_like(poles32)
    for b in range(pieces):
        got = blocks[b]
        point = [got[c] - CENTRE for c in range(3)]
        area = got[3]
        area = jnp.where(area > 0.0, area, 1.0)
        split = [thirds(p)[0:2] for p in point]
        square = point[0] * point[0] + point[1] * point[1] + point[2] * point[2]
        rows = [split[c][q] for c in range(3) for (_, q) in pairs]
        place(source32, b * leaves, rows + list(thirds(square + area)) + [ones] * 3)
        if b == 0:
            rows = [split[c][p] * (-2.0) for c in range(3) for (p, _) in pairs]
            place(target32, 0, rows + [ones] * 3 + list(thirds(square)))
        charge[pl.ds(b * leaves, leaves), :] = got[4]
        poles32[pl.ds(b * leaves, leaves), :] = got[5]
    source16[...] = source32[...].astype(bf16)
    for leaf in range(leaves):
        target16[leaf] = target32[leaf * WIDTH : (leaf + 1) * WIDTH, :].T.astype(bf16)
    pole = poles32[...]
    high = pole.astype(bf16)
    poles16 = jnp.concatenate([high, (pole - high.astype(f32)).astype(bf16)], axis=1)

    neighbours = near.shape[1]

    def near_body(leaf):
        total = jnp.zeros((panels, panels), f32)
        for start in range(0, neighbours, 2):
            ids = [near[leaf, e] for e in range(start, min(start + 2, neighbours))]
            source = [source16[pl.ds(pl.multiple_of(s * WIDTH, WIDTH), WIDTH), :] for s in ids]
            source = jnp.concatenate(source, axis=1) if len(ids) > 1 else source[0]
            inverse = lax.rsqrt(jnp.dot(target16[leaf], source, preferred_element_type=f32))
            for e, s in enumerate(ids):
                total += inverse[:, e * panels : (e + 1) * panels] * charge[pl.ds(s, 1), :]
        totals[leaf] = total

    def leaf_body(leaf):
        near_body(leaf)
        both = jnp.dot(hits[leaf], poles16, preferred_element_type=f32)
        found[leaf] = both[:, 0:panels] + both[:, panels : 2 * panels]

    for copy in copies[:tallies]:
        copy.wait()
    repeat(leaves, 4, leaf_body)
    nearby = jnp.concatenate(
        [jnp.sum(totals[leaf].T, axis=0, keepdims=True) for leaf in range(leaves)], axis=0
    )
    copies[tallies].wait()

    group = 8
    filler = jnp.zeros((terms * group, panels - terms), bf16)

    def translate(table, at):
        part = found[:, pl.ds(at, group), :].reshape(leaves * group, panels)
        first = part.astype(bf16)
        second = (part - first.astype(f32)).astype(bf16)
        table = jnp.concatenate([table.reshape(terms * group, terms), filler], axis=1)
        return lax.dot_general(
            jnp.concatenate([table, table], axis=1),
            jnp.concatenate([first, second], axis=1),
            across,
            preferred_element_type=f32,
        )

    full = offsets // group
    rest = offsets % group
    sums[...] = jnp.zeros_like(sums)
    if rest:
        tail = m2l[:, full * group : offsets, :].astype(f32)
        tail = jnp.concatenate([tail, jnp.zeros((terms, group - rest, terms), f32)], axis=1)
        sums[...] = translate(tail.reshape(terms * group, terms).astype(bf16), full * group)
    batch = next(n for n in range(min(13, full), 0, -1) if full % n == 0)

    def far_body(step, carry):
        value = None
        for i in range(batch):
            at = pl.multiple_of((step * batch + i) * group, group)
            one = translate(m2l[:, pl.ds(at, group), :], at)
            value = one if value is None else value + one
        sums[...] += value
        return carry

    lax.fori_loop(0, full // batch, far_body, 0)
    spread = leaves * group
    row = lax.broadcasted_iota(jnp.int32, (terms * group, spread), 0) & (group - 1)
    lane = lax.broadcasted_iota(jnp.int32, (terms * group, spread), 1) & (group - 1)
    kept = jnp.where(row == lane, sums[...], 0.0)
    kept = jnp.sum(kept.reshape(terms, group, spread), axis=1)
    owner = lax.broadcasted_iota(jnp.int32, (leaves, spread), 0) * group
    lane = lax.broadcasted_iota(jnp.int32, (leaves, spread), 1)
    pick = ((lane >= owner) & (lane < owner + group)).astype(f32).astype(bf16)
    local = jnp.zeros((leaves, terms), f32)
    for part in thirds(kept):
        local += lax.dot_general(pick, part.astype(bf16), across, preferred_element_type=f32)
    local = local.astype(bf16).astype(f32)
    distant = zeros
    for k in range(terms):
        distant += l2p[k].astype(f32) * local[:, k : k + 1]

    live = live_rows(counts, (leaves, panels))
    current = basis[krylov - 1] * live
    image = (0.5 * current + nearby + distant) * live
    image_out[...] = image
    rows = [jnp.sum(basis[j] * live * image, axis=0, keepdims=True) for j in range(krylov)]
    product = jnp.sum(jnp.concatenate(rows, axis=0), axis=1, keepdims=True)
    energy = jnp.sum(jnp.sum(image * image, axis=0, keepdims=True), axis=1, keepdims=True)
    lane = lax.broadcasted_iota(jnp.int32, (krylov, panels), 1)
    tile_out[...] = jnp.where(lane == 0, product, jnp.where(lane == 1, energy, gram[...]))


def repeat(count, most, body):
    batch = next(n for n in range(most, 0, -1) if count % n == 0)

    def several(step, carry):
        for i in range(batch):
            body(step * batch + i)
        return carry

    lax.fori_loop(0, count // batch, several, 0)


def final_kernel(counts, basis, image, tile, other, vector, column):
    krylov, leaves, panels = basis.shape
    sums = tile[...] + other[...]
    population = sums[0:1, 2:3]
    energy = sums[0:1, 1:2]
    products = sums[:, 0:1]
    coefficients = products / population
    row = lax.broadcasted_iota(jnp.int32, (krylov, panels), 0)
    lane = lax.broadcasted_iota(jnp.int32, (krylov, panels), 1)
    in_gram = (lane >= krylov) & (lane < 2 * krylov)
    applied = jnp.sum(jnp.where(in_gram, coefficients * sums, 0.0), axis=0, keepdims=True)
    across_lanes = jnp.sum(jnp.where(lane == krylov + row, coefficients, 0.0), axis=0, keepdims=True)
    curvature = jnp.sum(applied * across_lanes, axis=1, keepdims=True)
    crossed = jnp.sum(coefficients * products, axis=0, keepdims=True)
    squares = energy - 2.0 * crossed + curvature
    scale = jnp.sqrt(squares / population + epsilon)
    live = live_rows(counts, (leaves, panels))
    residue = image[...]
    for j in range(krylov):
        residue = residue - coefficients[j : j + 1, 0:1] * (basis[j] * live)
    vector[...] = residue / scale
    placed = jnp.sum(jnp.where(lane == row, coefficients, 0.0), axis=0, keepdims=True)
    placed = jnp.where(lane[0:1] == krylov, scale, placed)
    column[...] = placed.reshape(panels)[0 : krylov + 1]


def swap(value, axis, bit):
    count = lax.axis_size(axis)
    return lax.ppermute(value, axis, [(i, i ^ bit) for i in range(count)])


def hop(value, axis):
    count = lax.axis_size(axis)
    moves = [(i, i + 2 if i % 2 == 0 else i - 2) for i in range(count)]
    return lax.ppermute(value, axis, [(i, k) for i, k in moves if 0 <= k < count])


def on_device(basis, coords, areas, p2m, l2p, m2l, counts, near_list, far_list, far_offset):
    krylov, leaves, panels = basis.shape
    coords = jnp.transpose(coords, (1, 0, 2))
    p2m = jnp.transpose(p2m, (1, 0, 2))
    l2p = jnp.transpose(l2p, (2, 0, 1))
    m2l = jnp.transpose(m2l, (1, 0, 2))
    terms, offsets = m2l.shape[:2]
    groups = lax.axis_size("grp")
    params = pltpu.CompilerParams(vmem_limit_bytes=LIMIT)
    even = 1 - lax.axis_index("seg") % 2
    position = jnp.stack([lax.axis_index("grp"), 1 + even]).astype(jnp.int32)

    block = pl.pallas_call(
        prep_kernel,
        out_shape=jax.ShapeDtypeStruct((6, leaves, panels), f32),
        in_specs=smem(1) + vmem(4),
        out_specs=pl.BlockSpec(memory_space=pltpu.VMEM),
        compiler_params=params,
        name="prep",
    )(counts, basis, coords, areas, p2m)

    window = 3 * groups * leaves
    wide = window + -window % 128
    entries = far_list.shape[1] + -far_list.shape[1] % 128
    padded = offsets + -offsets % 16
    tallies = 3 if leaves % 3 == 0 else 1
    held = leaves // tallies

    def tally(index, after):
        return pl.pallas_call(
            functools.partial(tally_kernel, groups, leaves, index * held),
            out_shape=jax.ShapeDtypeStruct((held, padded, wide), bf16),
            in_specs=[pl.BlockSpec(memory_space=pl.ANY)] + smem(1) + vmem(2),
            out_specs=pl.BlockSpec(memory_space=pltpu.VMEM),
            scratch_shapes=[pltpu.VMEM((held, entries), jnp.int32)] * 2,
            compiler_params=params,
            name="tally",
        )(after, position, far_list, far_offset)

    def spread(value):
        whole = [value]
        bit = 2
        while bit < groups:
            whole = whole + [swap(v, "grp", bit) for v in whole]
            bit *= 2
        return whole

    beside = swap(block, "seg", 1)
    own = spread(block)
    hits = [tally(0, block)]
    beside, hits[0] = lax.optimization_barrier((beside, hits[0]))
    beyond = hop(beside, "seg")
    if tallies > 1:
        hits.append(tally(1, beside))
        beyond, hits[1] = lax.optimization_barrier((beyond, hits[1]))
        hits.append(tally(2, beyond))
    near_slots, gram = pl.pallas_call(
        functools.partial(plan_kernel, groups),
        out_shape=(
            jax.ShapeDtypeStruct(near_list.shape, jnp.int32),
            jax.ShapeDtypeStruct((krylov, panels), f32),
        ),
        in_specs=smem(2) + vmem(2),
        out_specs=tuple(vmem(2)),
        compiler_params=params,
        name="plan",
    )(counts, position, basis, near_list)
    here = own + spread(beside) + spread(beyond)
    blocks = here + [swap(v, "grp", 1) for v in here]

    image, tile = pl.pallas_call(
        functools.partial(main_kernel, len(blocks), tallies),
        out_shape=(
            jax.ShapeDtypeStruct((leaves, panels), f32),
            jax.ShapeDtypeStruct((krylov, panels), f32),
        ),
        in_specs=smem(2)
        + vmem(len(blocks))
        + [pl.BlockSpec(memory_space=pl.ANY)] * (tallies + 1)
        + vmem(3),
        out_specs=tuple(vmem(2)),
        scratch_shapes=[
            pltpu.VMEM((leaves, padded, wide), bf16),
            pltpu.VMEM(m2l.shape, bf16),
            pltpu.VMEM((window * WIDTH, panels), f32),
            pltpu.VMEM((window * WIDTH, panels), bf16),
            pltpu.VMEM((leaves * WIDTH, panels), f32),
            pltpu.VMEM((leaves, panels, WIDTH), bf16),
            pltpu.VMEM((window, panels), f32),
            pltpu.VMEM((wide, panels), f32),
            pltpu.VMEM((terms * 8, leaves * 8), f32),
            pltpu.VMEM((leaves, panels, panels), f32),
            pltpu.VMEM((leaves, padded, panels), f32),
            pltpu.SemaphoreType.DMA((tallies + 1,)),
        ],
        compiler_params=params,
        name="main",
    )(counts, near_slots, *blocks, *hits, m2l, l2p, basis, gram)

    stages = [
        (axis, 1 << power)
        for axis in ("grp", "seg")
        for power in range((lax.axis_size(axis) - 1).bit_length())
    ]
    for axis, bit in stages[:-1]:
        tile = tile + swap(tile, axis, bit)
    other = swap(tile, *stages[-1])

    return pl.pallas_call(
        final_kernel,
        out_shape=(
            jax.ShapeDtypeStruct((leaves, panels), f32),
            jax.ShapeDtypeStruct((krylov + 1,), f32),
        ),
        in_specs=smem(1) + vmem(4),
        out_specs=tuple(vmem(2)),
        compiler_params=params,
        name="final",
    )(counts, basis, image, tile, other)


def solution(mesh):
    placed = (
        P(None, ("seg", "grp"), None),
        P(("seg", "grp"), None, None),
        P(("seg", "grp"), None),
        P(("seg", "grp"), None, None),
        P(("seg", "grp"), None, None),
        P(),
        P(("seg", "grp")),
        P(("seg", "grp"), None),
        P(("seg", "grp"), None),
        P(("seg", "grp"), None),
    )
    return jax.shard_map(
        on_device,
        mesh=mesh,
        in_specs=placed,
        out_specs=(P(("seg", "grp"), None), P()),
        check_vma=False,
    )
```

```python
import functools

import jax
import jax.numpy as jnp
from jax import lax
from jax.experimental import pallas as pl
from jax.experimental.pallas import tpu as pltpu
from jax.sharding import PartitionSpec as P

four_pi = 12.566370614359172
epsilon = 1e-06
bf16 = jnp.bfloat16
f32 = jnp.float32
WIDTH = 16
CENTRE = 2.0
UNROLL = 4
LIMIT = 56 * 1024 * 1024

across = (((1,), (1,)), ((), ()))


def vmem(count):
    return [pl.BlockSpec(memory_space=pltpu.VMEM)] * count


def smem(count):
    return [pl.BlockSpec(memory_space=pltpu.SMEM)] * count


def live_rows(counts, shape):
    return (lax.broadcasted_iota(jnp.int32, shape, 0) < counts[0]).astype(f32)


def prep_kernel(counts, basis, coords, areas, p2m, block):
    leaves, panels = areas.shape
    terms = p2m.shape[0]
    current = basis[basis.shape[0] - 1] * live_rows(counts, (leaves, panels))
    rounded = current.astype(bf16).astype(f32)
    lane = lax.broadcasted_iota(jnp.int32, (leaves, panels), 1)
    poles = jnp.zeros((leaves, panels), f32)
    for k in range(terms):
        moved = jnp.sum(p2m[k].astype(f32) * rounded, axis=1, keepdims=True)
        poles = jnp.where(lane == k, moved, poles)
    for c in range(3):
        block[c] = coords[c]
    block[3] = areas[...]
    block[4] = areas[...] * current * (1.0 / four_pi)
    block[5] = poles


def slot_of(window, table, leaves, me, order_low):
    groups = len(table[0])
    span = groups * leaves
    low = (window < span).astype(jnp.int32)
    high = (window >= 2 * span).astype(jnp.int32)
    order = low * order_low + high * (3 - order_low)
    inner = window - span * (1 - low + high)
    group = jnp.zeros_like(window)
    for g in range(1, groups):
        group += (inner >= g * leaves).astype(jnp.int32)
    key = order * groups + (group ^ me)
    column = jnp.zeros_like(window)
    for i, line in enumerate(table):
        for j, at in enumerate(line):
            column = jnp.where(key == i * groups + j, at, column)
    return column * leaves + inner - group * leaves


def plan_kernel(table, counts, place, basis, near, far, near_slots, far_slots, gram):
    krylov, leaves, panels = basis.shape
    near_slots[...] = slot_of(near[...], table, leaves, place[0], place[1])
    far_slots[...] = slot_of(far[...], table, leaves, place[0], place[1])
    live = live_rows(counts, (leaves, panels))
    masked = [basis[j] * live for j in range(krylov)]
    lane = lax.broadcasted_iota(jnp.int32, (krylov, panels), 1)
    tile = jnp.zeros((krylov, panels), f32)
    for j in range(krylov):
        rows_j = [jnp.sum(masked[i] * masked[j], axis=0, keepdims=True) for i in range(krylov)]
        column = jnp.sum(jnp.concatenate(rows_j, axis=0), axis=1, keepdims=True)
        tile = jnp.where(lane == krylov + j, column, tile)
    population = (jnp.minimum(counts[0], leaves) * panels).astype(f32)
    gram[...] = jnp.where(lane == 2, population, tile)


def thirds(value):
    first = value.astype(bf16).astype(f32)
    second = (value - first).astype(bf16).astype(f32)
    return first, second, value - first - second


pairs = ((0, 0), (0, 1), (1, 0))


def main_kernel(orders, *refs):
    pieces = len(orders)
    counts, place, near, far = refs[0:4]
    blocks = refs[4 : 4 + pieces]
    classes, m2l_hbm, l2p, basis, gram, image_out, tile_out = refs[4 + pieces : 11 + pieces]
    m2l, source32, source16, target32, target16 = refs[11 + pieces : 16 + pieces]
    charge, poles32, taken, sums, totals, found, sem = refs[16 + pieces :]
    krylov, leaves, panels = basis.shape
    terms = l2p.shape[0]
    offsets = m2l.shape[1]
    copy = pltpu.make_async_copy(m2l_hbm, m2l, sem)
    copy.start()
    inside = place[2].astype(f32)

    ones = jnp.ones((leaves, panels), f32)
    zeros = jnp.zeros((leaves, panels), f32)

    def lay(ref, base, rows):
        for k in range(WIDTH):
            value = rows[k] if k < len(rows) else zeros
            ref[pl.ds(base * WIDTH + k, leaves, stride=WIDTH), :] = value

    for b in range(pieces):
        got = blocks[b]
        point = [got[c] - CENTRE for c in range(3)]
        area = got[3]
        area = jnp.where(area > 0.0, area, 1.0)
        split = [thirds(p)[0:2] for p in point]
        square = point[0] * point[0] + point[1] * point[1] + point[2] * point[2]
        rows = [split[c][q] for c in range(3) for (_, q) in pairs]
        lay(source32, b * leaves, rows + list(thirds(square + area)) + [ones] * 3)
        if b == 0:
            rows = [split[c][p] * (-2.0) for c in range(3) for (p, _) in pairs]
            lay(target32, 0, rows + [ones] * 3 + list(thirds(square)))
        known = inside if orders[b] == 2 else 1.0
        charge[pl.ds(b * leaves, leaves), :] = got[4] * known
        poles32[pl.ds(b * leaves, leaves), :] = got[5] * known
    source16[...] = source32[...].astype(bf16)
    for leaf in range(leaves):
        target16[leaf] = target32[leaf * WIDTH : (leaf + 1) * WIDTH, :].T.astype(bf16)
    neighbours = near.shape[1]

    entries = far.shape[1]
    padded = found.shape[1]
    depth = taken.shape[1]
    taken[:, entries:, :] = jnp.zeros((taken.shape[0], depth - entries, panels), f32)

    def leaf_body(leaf, i):
        for e in range(entries):
            taken[i, e : e + 1, :] = poles32[pl.ds(far[leaf, e], 1), :]
        total = jnp.zeros((panels, panels), f32)
        for start in range(0, neighbours, 2):
            ids = [near[leaf, e] for e in range(start, min(start + 2, neighbours))]
            source = [source16[pl.ds(pl.multiple_of(s * WIDTH, WIDTH), WIDTH), :] for s in ids]
            source = jnp.concatenate(source, axis=1) if len(ids) > 1 else source[0]
            inverse = lax.rsqrt(jnp.dot(target16[leaf], source, preferred_element_type=f32))
            for e, s in enumerate(ids):
                total += inverse[:, e * panels : (e + 1) * panels] * charge[pl.ds(s, 1), :]
        totals[leaf] = total
        pole = taken[i]
        high = pole.astype(bf16)
        pole = jnp.concatenate([high, (pole - high.astype(f32)).astype(bf16)], axis=1)
        offset = classes[pl.ds(leaf, 1), :]
        by_class = lax.broadcasted_iota(jnp.int32, (padded, entries), 0) == offset
        by_class = jnp.concatenate(
            [by_class.astype(f32), jnp.zeros((padded, depth - entries), f32)], axis=1
        ).astype(bf16)
        both = jnp.dot(by_class, pole, preferred_element_type=f32)
        found[leaf] = both[:, 0:panels] + both[:, panels : 2 * panels]

    repeat(leaves, UNROLL, leaf_body)
    nearby = jnp.concatenate(
        [jnp.sum(totals[leaf].T, axis=0, keepdims=True) for leaf in range(leaves)], axis=0
    )
    copy.wait()

    group = 8
    filler = jnp.zeros((terms * group, panels - terms), bf16)

    def translate(table, at):
        part = found[:, pl.ds(at, group), :].reshape(leaves * group, panels)
        first = part.astype(bf16)
        second = (part - first.astype(f32)).astype(bf16)
        table = jnp.concatenate([table.reshape(terms * group, terms), filler], axis=1)
        return lax.dot_general(
            jnp.concatenate([table, table], axis=1),
            jnp.concatenate([first, second], axis=1),
            across,
            preferred_element_type=f32,
        )

    full = offsets // group
    rest = offsets % group
    sums[...] = jnp.zeros_like(sums)
    if rest:
        tail = m2l[:, full * group : offsets, :].astype(f32)
        tail = jnp.concatenate([tail, jnp.zeros((terms, group - rest, terms), f32)], axis=1)
        sums[...] = translate(tail.reshape(terms * group, terms).astype(bf16), full * group)
    batch = next(n for n in range(min(13, full), 0, -1) if full % n == 0)

    def far_body(step, carry):
        value = None
        for i in range(batch):
            at = pl.multiple_of((step * batch + i) * group, group)
            one = translate(m2l[:, pl.ds(at, group), :], at)
            value = one if value is None else value + one
        sums[...] += value
        return carry

    lax.fori_loop(0, full // batch, far_body, 0)
    spread = leaves * group
    row = lax.broadcasted_iota(jnp.int32, (terms * group, spread), 0) & (group - 1)
    lane = lax.broadcasted_iota(jnp.int32, (terms * group, spread), 1) & (group - 1)
    kept = jnp.where(row == lane, sums[...], 0.0)
    kept = jnp.sum(kept.reshape(terms, group, spread), axis=1)
    owner = lax.broadcasted_iota(jnp.int32, (leaves, spread), 0) * group
    lane = lax.broadcasted_iota(jnp.int32, (leaves, spread), 1)
    pick = ((lane >= owner) & (lane < owner + group)).astype(f32).astype(bf16)
    local = jnp.zeros((leaves, terms), f32)
    for part in thirds(kept):
        local += lax.dot_general(pick, part.astype(bf16), across, preferred_element_type=f32)
    local = local.astype(bf16).astype(f32)
    distant = zeros
    for k in range(terms):
        distant += l2p[k].astype(f32) * local[:, k : k + 1]

    live = live_rows(counts, (leaves, panels))
    current = basis[krylov - 1] * live
    image = (0.5 * current + nearby + distant) * live
    image_out[...] = image
    rows = [jnp.sum(basis[j] * live * image, axis=0, keepdims=True) for j in range(krylov)]
    product = jnp.sum(jnp.concatenate(rows, axis=0), axis=1, keepdims=True)
    energy = jnp.sum(jnp.sum(image * image, axis=0, keepdims=True), axis=1, keepdims=True)
    lane = lax.broadcasted_iota(jnp.int32, (krylov, panels), 1)
    tile_out[...] = jnp.where(lane == 0, product, jnp.where(lane == 1, energy, gram[...]))


def repeat(count, most, body):
    batch = next(n for n in range(most, 0, -1) if count % n == 0)

    def several(step, carry):
        for i in range(batch):
            body(step * batch + i, i)
        return carry

    lax.fori_loop(0, count // batch, several, 0)


def final_kernel(counts, basis, image, tile, other, vector, column):
    krylov, leaves, panels = basis.shape
    sums = tile[...] + other[...]
    population = sums[0:1, 2:3]
    energy = sums[0:1, 1:2]
    products = sums[:, 0:1]
    coefficients = products / population
    row = lax.broadcasted_iota(jnp.int32, (krylov, panels), 0)
    lane = lax.broadcasted_iota(jnp.int32, (krylov, panels), 1)
    in_gram = (lane >= krylov) & (lane < 2 * krylov)
    applied = jnp.sum(jnp.where(in_gram, coefficients * sums, 0.0), axis=0, keepdims=True)
    across_lanes = jnp.sum(jnp.where(lane == krylov + row, coefficients, 0.0), axis=0, keepdims=True)
    curvature = jnp.sum(applied * across_lanes, axis=1, keepdims=True)
    crossed = jnp.sum(coefficients * products, axis=0, keepdims=True)
    squares = energy - 2.0 * crossed + curvature
    scale = jnp.sqrt(squares / population + epsilon)
    live = live_rows(counts, (leaves, panels))
    residue = image[...]
    for j in range(krylov):
        residue = residue - coefficients[j : j + 1, 0:1] * (basis[j] * live)
    vector[...] = residue / scale
    placed = jnp.sum(jnp.where(lane == row, coefficients, 0.0), axis=0, keepdims=True)
    placed = jnp.where(lane[0:1] == krylov, scale, placed)
    column[...] = placed.reshape(panels)[0 : krylov + 1]


def move(value, step):
    segments, groups = lax.axis_size("seg"), lax.axis_size("grp")
    moves = []
    for segment in range(segments):
        for group in range(groups):
            to = step(segment, group)
            moves.append((segment * groups + group, to[0] * groups + to[1]))
    return lax.ppermute(value, ("seg", "grp"), moves)


def swap(value, segment_bit, group_bit):
    return move(value, lambda s, g: (s ^ segment_bit, g ^ group_bit))


def hop(value):
    segments = lax.axis_size("seg")

    def step(s, g):
        to = s + 2 if s % 2 == 0 else s - 2
        return (to if 0 <= to < segments else s ^ 1, g ^ 1)

    return move(value, step)


def on_device(basis, coords, areas, p2m, l2p, m2l, counts, near_list, far_list, far_offset):
    krylov, leaves, panels = basis.shape
    coords = jnp.transpose(coords, (1, 0, 2))
    p2m = jnp.transpose(p2m, (1, 0, 2))
    l2p = jnp.transpose(l2p, (2, 0, 1))
    m2l = jnp.transpose(m2l, (1, 0, 2))
    terms, offsets = m2l.shape[:2]
    groups = lax.axis_size("grp")
    params = pltpu.CompilerParams(vmem_limit_bytes=LIMIT)
    here = lax.axis_index("seg")
    odd = here % 2
    order_low = 2 - odd
    inside = jnp.where(odd == 0, here >= 2, here < lax.axis_size("seg") - 2)
    position = jnp.stack([lax.axis_index("grp"), order_low, inside]).astype(jnp.int32)

    block = pl.pallas_call(
        prep_kernel,
        out_shape=jax.ShapeDtypeStruct((6, leaves, panels), f32),
        in_specs=smem(1) + vmem(4),
        out_specs=pl.BlockSpec(memory_space=pltpu.VMEM),
        compiler_params=params,
        name="prep",
    )(counts, basis, coords, areas, p2m)

    window = 3 * groups * leaves
    entries = far_list.shape[1]
    padded = offsets + -offsets % 16

    def spread(pieces):
        bit = 2
        while bit < groups:
            mask = bit | 1
            pieces = pieces + [(swap(v, 0, mask), order, rel ^ mask) for v, order, rel in pieces]
            bit *= 2
        return pieces

    beside = swap(block, 1, 1)
    own = spread([(block, 0, 0)])
    beyond = hop(beside)
    pieces = own + [(beside, 1, 1)] + [(swap(v, 1, 1), 1, rel ^ 1) for v, _, rel in own[1:]]
    pieces = pieces + spread([(beyond, 2, 0)])
    pieces = pieces + [(swap(v, 0, 1), order, rel ^ 1) for v, order, rel in pieces]
    table = [[0] * groups for _ in range(3)]
    for at, (_, order, rel) in enumerate(pieces):
        table[order][rel] = at
    near_slots, far_slots, gram = pl.pallas_call(
        functools.partial(plan_kernel, table),
        out_shape=(
            jax.ShapeDtypeStruct(near_list.shape, jnp.int32),
            jax.ShapeDtypeStruct(far_list.shape, jnp.int32),
            jax.ShapeDtypeStruct((krylov, panels), f32),
        ),
        in_specs=smem(2) + vmem(3),
        out_specs=tuple(vmem(3)),
        compiler_params=params,
        name="plan",
    )(counts, position, basis, near_list, far_list)

    image, tile = pl.pallas_call(
        functools.partial(main_kernel, [order for _, order, _ in pieces]),
        out_shape=(
            jax.ShapeDtypeStruct((leaves, panels), f32),
            jax.ShapeDtypeStruct((krylov, panels), f32),
        ),
        in_specs=smem(4)
        + vmem(len(pieces) + 1)
        + [pl.BlockSpec(memory_space=pl.ANY)]
        + vmem(3),
        out_specs=tuple(vmem(2)),
        scratch_shapes=[
            pltpu.VMEM(m2l.shape, bf16),
            pltpu.VMEM((window * WIDTH, panels), f32),
            pltpu.VMEM((window * WIDTH, panels), bf16),
            pltpu.VMEM((leaves * WIDTH, panels), f32),
            pltpu.VMEM((leaves, panels, WIDTH), bf16),
            pltpu.VMEM((window, panels), f32),
            pltpu.VMEM((window, panels), f32),
            pltpu.VMEM((UNROLL, entries + -entries % 64, panels), f32),
            pltpu.VMEM((terms * 8, leaves * 8), f32),
            pltpu.VMEM((leaves, panels, panels), f32),
            pltpu.VMEM((leaves, padded, panels), f32),
            pltpu.SemaphoreType.DMA,
        ],
        compiler_params=params,
        name="main",
    )(
        counts, position, near_slots, far_slots,
        *[v for v, _, _ in pieces], far_offset, m2l, l2p, basis, gram,
    )

    def masks(axis):
        return [1 << power for power in range((lax.axis_size(axis) - 1).bit_length())]

    stages = [(0, bit if bit == 1 else bit | 1) for bit in masks("grp")]
    stages += [(bit, 1) for bit in masks("seg")]
    for stage in stages[:-1]:
        tile = tile + swap(tile, *stage)
    other = swap(tile, *stages[-1])

    return pl.pallas_call(
        final_kernel,
        out_shape=(
            jax.ShapeDtypeStruct((leaves, panels), f32),
            jax.ShapeDtypeStruct((krylov + 1,), f32),
        ),
        in_specs=smem(1) + vmem(4),
        out_specs=tuple(vmem(2)),
        compiler_params=params,
        name="final",
    )(counts, basis, image, tile, other)


def solution(mesh):
    placed = (
        P(None, ("seg", "grp"), None),
        P(("seg", "grp"), None, None),
        P(("seg", "grp"), None),
        P(("seg", "grp"), None, None),
        P(("seg", "grp"), None, None),
        P(),
        P(("seg", "grp")),
        P(("seg", "grp"), None),
        P(("seg", "grp"), None),
        P(("seg", "grp"), None),
    )
    return jax.shard_map(
        on_device,
        mesh=mesh,
        in_specs=placed,
        out_specs=(P(("seg", "grp"), None), P()),
        check_vma=False,
    )
```

```python
import functools

import jax
import jax.numpy as jnp
from jax import lax
from jax.experimental import pallas as pl
from jax.experimental.pallas import tpu as pltpu
from jax.sharding import PartitionSpec as P

four_pi = 12.566370614359172
epsilon = 1e-06
bf16 = jnp.bfloat16
f32 = jnp.float32
WIDTH = 16
CENTRE = 2.0
UNROLL = 8
LIMIT = 56 * 1024 * 1024

across = (((1,), (1,)), ((), ()))


def vmem(count):
    return [pl.BlockSpec(memory_space=pltpu.VMEM)] * count


def anywhere(count):
    return [pl.BlockSpec(memory_space=pl.ANY)] * count


def smem(count):
    return [pl.BlockSpec(memory_space=pltpu.SMEM)] * count


def live_rows(counts, shape):
    return (lax.broadcasted_iota(jnp.int32, shape, 0) < counts[0]).astype(f32)


def prep_kernel(counts, basis, coords, areas, p2m, block):
    leaves, panels = areas.shape
    terms = p2m.shape[0]
    current = basis[basis.shape[0] - 1] * live_rows(counts, (leaves, panels))
    rounded = current.astype(bf16).astype(f32)
    lane = lax.broadcasted_iota(jnp.int32, (leaves, panels), 1)
    poles = jnp.zeros((leaves, panels), f32)
    for k in range(terms):
        moved = jnp.sum(p2m[k].astype(f32) * rounded, axis=1, keepdims=True)
        poles = jnp.where(lane == k, moved, poles)
    for c in range(3):
        block[c] = coords[c]
    block[3] = areas[...]
    block[4] = areas[...] * current * (1.0 / four_pi)
    block[5] = poles


def slot_of(window, table, leaves, me, order_low):
    groups = len(table[0])
    span = groups * leaves
    low = (window < span).astype(jnp.int32)
    high = (window >= 2 * span).astype(jnp.int32)
    order = low * order_low + high * (3 - order_low)
    inner = window - span * (1 - low + high)
    group = jnp.zeros_like(window)
    for g in range(1, groups):
        group += (inner >= g * leaves).astype(jnp.int32)
    key = order * groups + (group ^ me)
    column = jnp.zeros_like(window)
    for i, line in enumerate(table):
        for j, at in enumerate(line):
            column = jnp.where(key == i * groups + j, at, column)
    return column * leaves + inner - group * leaves


def plan_kernel(table, counts, place, basis, near, far, near_slots, far_slots, gram):
    krylov, leaves, panels = basis.shape
    near_slots[...] = slot_of(near[...], table, leaves, place[0], place[1])
    far_slots[...] = slot_of(far[...], table, leaves, place[0], place[1])
    live = live_rows(counts, (leaves, panels))
    masked = [basis[j] * live for j in range(krylov)]
    lane = lax.broadcasted_iota(jnp.int32, (krylov, panels), 1)
    tile = jnp.zeros((krylov, panels), f32)
    for j in range(krylov):
        rows_j = [jnp.sum(masked[i] * masked[j], axis=0, keepdims=True) for i in range(krylov)]
        column = jnp.sum(jnp.concatenate(rows_j, axis=0), axis=1, keepdims=True)
        tile = jnp.where(lane == krylov + j, column, tile)
    population = (jnp.minimum(counts[0], leaves) * panels).astype(f32)
    gram[...] = jnp.where(lane == 2, population, tile)


def thirds(value):
    first = value.astype(bf16).astype(f32)
    second = (value - first).astype(bf16).astype(f32)
    return first, second, value - first - second


pairs = ((0, 0), (0, 1), (1, 0))


def main_kernel(orders, *refs):
    pieces = len(orders)
    counts, place, near, far = refs[0:4]
    blocks = refs[4 : 4 + pieces]
    classes, m2l_hbm, l2p, basis, gram, image_out, tile_out = refs[4 + pieces : 11 + pieces]
    m2l, source32, source16, target32, target16 = refs[11 + pieces : 16 + pieces]
    charge, poles32, taken, sums, totals, found, sem = refs[16 + pieces :]
    krylov, leaves, panels = basis.shape
    terms = l2p.shape[0]
    offsets = m2l.shape[1]
    copy = pltpu.make_async_copy(m2l_hbm, m2l, sem)
    copy.start()
    inside = place[2].astype(f32)

    ones = jnp.ones((leaves, panels), f32)
    zeros = jnp.zeros((leaves, panels), f32)

    def lay(ref, base, rows):
        for k in range(WIDTH):
            value = rows[k] if k < len(rows) else zeros
            ref[pl.ds(base * WIDTH + k, leaves, stride=WIDTH), :] = value

    for b in range(pieces):
        got = blocks[b]
        point = [got[c] - CENTRE for c in range(3)]
        area = got[3]
        area = jnp.where(area > 0.0, area, 1.0)
        split = [thirds(p)[0:2] for p in point]
        square = point[0] * point[0] + point[1] * point[1] + point[2] * point[2]
        rows = [split[c][q] for c in range(3) for (_, q) in pairs]
        lay(source32, b * leaves, rows + list(thirds(square + area)) + [ones] * 3)
        if b == 0:
            rows = [split[c][p] * (-2.0) for c in range(3) for (p, _) in pairs]
            lay(target32, 0, rows + [ones] * 3 + list(thirds(square)))
        known = inside if orders[b] == 2 else 1.0
        charge[pl.ds(b * leaves, leaves), :] = got[4] * known
        poles32[pl.ds(b * leaves, leaves), :] = got[5] * known
    source16[...] = source32[...].astype(bf16)
    for leaf in range(leaves):
        target16[leaf] = target32[leaf * WIDTH : (leaf + 1) * WIDTH, :].T.astype(bf16)
    neighbours = near.shape[1]

    entries = far.shape[1]
    padded = found.shape[1]
    depth = taken.shape[1]
    taken[:, entries:, :] = jnp.zeros((taken.shape[0], depth - entries, panels), f32)

    def near_body(leaf, i):
        total = jnp.zeros((panels, panels), f32)
        for start in range(0, neighbours, 2):
            ids = [near[leaf, e] for e in range(start, min(start + 2, neighbours))]
            source = [source16[pl.ds(pl.multiple_of(s * WIDTH, WIDTH), WIDTH), :] for s in ids]
            source = jnp.concatenate(source, axis=1) if len(ids) > 1 else source[0]
            inverse = lax.rsqrt(jnp.dot(target16[leaf], source, preferred_element_type=f32))
            for e, s in enumerate(ids):
                total += inverse[:, e * panels : (e + 1) * panels] * charge[pl.ds(s, 1), :]
        totals[leaf] = total

    def far_gather(leaf, i):
        for e in range(entries):
            taken[i, e : e + 1, :] = poles32[pl.ds(far[leaf, e], 1), :]
        pole = taken[i]
        high = pole.astype(bf16)
        pole = jnp.concatenate([high, (pole - high.astype(f32)).astype(bf16)], axis=1)
        offset = classes[pl.ds(leaf, 1), :]
        by_class = lax.broadcasted_iota(jnp.int32, (padded, entries), 0) == offset
        by_class = jnp.concatenate(
            [by_class.astype(f32), jnp.zeros((padded, depth - entries), f32)], axis=1
        ).astype(bf16)
        both = jnp.dot(by_class, pole, preferred_element_type=f32)
        found[leaf] = both[:, 0:panels] + both[:, panels : 2 * panels]

    repeat(leaves, 12, near_body)
    repeat(leaves, UNROLL, far_gather)
    nearby = jnp.concatenate(
        [jnp.sum(totals[leaf].T, axis=0, keepdims=True) for leaf in range(leaves)], axis=0
    )
    copy.wait()

    group = 8
    filler = jnp.zeros((terms * group, panels - terms), bf16)

    def translate(table, at):
        part = found[:, pl.ds(at, group), :].reshape(leaves * group, panels)
        first = part.astype(bf16)
        second = (part - first.astype(f32)).astype(bf16)
        table = jnp.concatenate([table.reshape(terms * group, terms), filler], axis=1)
        return lax.dot_general(
            jnp.concatenate([table, table], axis=1),
            jnp.concatenate([first, second], axis=1),
            across,
            preferred_element_type=f32,
        )

    full = offsets // group
    rest = offsets % group
    sums[...] = jnp.zeros_like(sums)
    if rest:
        tail = m2l[:, full * group : offsets, :].astype(f32)
        tail = jnp.concatenate([tail, jnp.zeros((terms, group - rest, terms), f32)], axis=1)
        sums[...] = translate(tail.reshape(terms * group, terms).astype(bf16), full * group)
    batch = next(n for n in range(min(39, full), 0, -1) if full % n == 0)

    def far_body(step, carry):
        value = None
        for i in range(batch):
            at = pl.multiple_of((step * batch + i) * group, group)
            one = translate(m2l[:, pl.ds(at, group), :], at)
            value = one if value is None else value + one
        sums[...] += value
        return carry

    lax.fori_loop(0, full // batch, far_body, 0)
    spread = leaves * group
    row = lax.broadcasted_iota(jnp.int32, (terms * group, spread), 0) & (group - 1)
    lane = lax.broadcasted_iota(jnp.int32, (terms * group, spread), 1) & (group - 1)
    kept = jnp.where(row == lane, sums[...], 0.0)
    kept = jnp.sum(kept.reshape(terms, group, spread), axis=1)
    owner = lax.broadcasted_iota(jnp.int32, (leaves, spread), 0) * group
    lane = lax.broadcasted_iota(jnp.int32, (leaves, spread), 1)
    pick = ((lane >= owner) & (lane < owner + group)).astype(f32).astype(bf16)
    local = jnp.zeros((leaves, terms), f32)
    for part in thirds(kept):
        local += lax.dot_general(pick, part.astype(bf16), across, preferred_element_type=f32)
    local = local.astype(bf16).astype(f32)
    distant = zeros
    for k in range(terms):
        distant += l2p[k].astype(f32) * local[:, k : k + 1]

    live = live_rows(counts, (leaves, panels))
    current = basis[krylov - 1] * live
    image = (0.5 * current + nearby + distant) * live
    image_out[...] = image
    rows = [jnp.sum(basis[j] * live * image, axis=0, keepdims=True) for j in range(krylov)]
    product = jnp.sum(jnp.concatenate(rows, axis=0), axis=1, keepdims=True)
    energy = jnp.sum(jnp.sum(image * image, axis=0, keepdims=True), axis=1, keepdims=True)
    lane = lax.broadcasted_iota(jnp.int32, (krylov, panels), 1)
    tile_out[...] = jnp.where(lane == 0, product, jnp.where(lane == 1, energy, gram[...]))


def repeat(count, most, body):
    batch = next(n for n in range(most, 0, -1) if count % n == 0)

    def several(step, carry):
        for i in range(batch):
            body(step * batch + i, i)
        return carry

    lax.fori_loop(0, count // batch, several, 0)


def final_kernel(counts, *refs):
    vector, column = refs[4:6]
    basis, image, tile, other = refs[6:10]
    sems = refs[10]
    copies = [pltpu.make_async_copy(refs[i], refs[6 + i], sems.at[i]) for i in range(4)]
    for copy in copies:
        copy.start()
    for copy in copies:
        copy.wait()
    krylov, leaves, panels = basis.shape
    sums = tile[...] + other[...]
    population = sums[0:1, 2:3]
    energy = sums[0:1, 1:2]
    products = sums[:, 0:1]
    coefficients = products / population
    row = lax.broadcasted_iota(jnp.int32, (krylov, panels), 0)
    lane = lax.broadcasted_iota(jnp.int32, (krylov, panels), 1)
    in_gram = (lane >= krylov) & (lane < 2 * krylov)
    applied = jnp.sum(jnp.where(in_gram, coefficients * sums, 0.0), axis=0, keepdims=True)
    across_lanes = jnp.sum(jnp.where(lane == krylov + row, coefficients, 0.0), axis=0, keepdims=True)
    curvature = jnp.sum(applied * across_lanes, axis=1, keepdims=True)
    crossed = jnp.sum(coefficients * products, axis=0, keepdims=True)
    squares = energy - 2.0 * crossed + curvature
    scale = jnp.sqrt(squares / population + epsilon)
    live = live_rows(counts, (leaves, panels))
    residue = image[...]
    for j in range(krylov):
        residue = residue - coefficients[j : j + 1, 0:1] * (basis[j] * live)
    vector[...] = residue / scale
    placed = jnp.sum(jnp.where(lane == row, coefficients, 0.0), axis=0, keepdims=True)
    placed = jnp.where(lane[0:1] == krylov, scale, placed)
    column[...] = placed.reshape(panels)[0 : krylov + 1]


def move(value, step):
    segments, groups = lax.axis_size("seg"), lax.axis_size("grp")
    moves = []
    for segment in range(segments):
        for group in range(groups):
            to = step(segment, group)
            moves.append((segment * groups + group, to[0] * groups + to[1]))
    return lax.ppermute(value, ("seg", "grp"), moves)


def swap(value, segment_bit, group_bit):
    return move(value, lambda s, g: (s ^ segment_bit, g ^ group_bit))


def hop(value):
    segments = lax.axis_size("seg")

    def step(s, g):
        to = s + 2 if s % 2 == 0 else s - 2
        return (to if 0 <= to < segments else s ^ 1, g ^ 1)

    return move(value, step)


def on_device(basis, coords, areas, p2m, l2p, m2l, counts, near_list, far_list, far_offset):
    krylov, leaves, panels = basis.shape
    coords = jnp.transpose(coords, (1, 0, 2))
    p2m = jnp.transpose(p2m, (1, 0, 2))
    l2p = jnp.transpose(l2p, (2, 0, 1))
    m2l = jnp.transpose(m2l, (1, 0, 2))
    terms, offsets = m2l.shape[:2]
    groups = lax.axis_size("grp")
    params = pltpu.CompilerParams(vmem_limit_bytes=LIMIT)
    small = pltpu.CompilerParams(vmem_limit_bytes=LIMIT // 8)
    here = lax.axis_index("seg")
    odd = here % 2
    order_low = 2 - odd
    inside = jnp.where(odd == 0, here >= 2, here < lax.axis_size("seg") - 2)
    position = jnp.stack([lax.axis_index("grp"), order_low, inside]).astype(jnp.int32)

    block = pl.pallas_call(
        prep_kernel,
        out_shape=jax.ShapeDtypeStruct((6, leaves, panels), f32),
        in_specs=smem(1) + vmem(4),
        out_specs=pl.BlockSpec(memory_space=pltpu.VMEM),
        compiler_params=params,
        name="prep",
    )(counts, basis, coords, areas, p2m)

    window = 3 * groups * leaves
    entries = far_list.shape[1]
    padded = offsets + -offsets % 16

    def spread(pieces):
        bit = 2
        while bit < groups:
            pieces = pieces + [swap(v, 0, bit | 1) for v in pieces]
            bit *= 2
        return pieces

    beside = swap(block, 1, 1)
    own = spread([block])
    rels = [0]
    bit = 2
    while bit < groups:
        rels = rels + [rel ^ bit ^ 1 for rel in rels]
        bit *= 2
    keys = [(0, rel) for rel in rels] + [(1, rel ^ 1) for rel in rels] + [(2, rel) for rel in rels]
    keys = keys + [(order, rel ^ 1) for order, rel in keys]
    table = [[keys.index((order, rel)) for rel in range(groups)] for order in range(3)]
    near_slots, far_slots, gram = pl.pallas_call(
        functools.partial(plan_kernel, table),
        out_shape=(
            jax.ShapeDtypeStruct(near_list.shape, jnp.int32),
            jax.ShapeDtypeStruct(far_list.shape, jnp.int32),
            jax.ShapeDtypeStruct((krylov, panels), f32),
        ),
        in_specs=smem(2) + vmem(3),
        out_specs=tuple(vmem(3)),
        compiler_params=params,
        name="plan",
    )(counts, position, basis, near_list, far_list)

    beside, near_slots = lax.optimization_barrier((beside, near_slots))
    beyond = hop(beside)
    pieces = own + [beside] + [swap(v, 1, 1) for v in own[1:]] + spread([beyond])
    pieces = pieces + [swap(v, 0, 1) for v in pieces]

    image, tile = pl.pallas_call(
        functools.partial(main_kernel, [order for order, _ in keys]),
        out_shape=(
            jax.ShapeDtypeStruct((leaves, panels), f32),
            jax.ShapeDtypeStruct((krylov, panels), f32),
        ),
        in_specs=smem(4) + vmem(len(pieces) + 1) + anywhere(1) + vmem(3),
        out_specs=tuple(vmem(2)),
        scratch_shapes=[
            pltpu.VMEM(m2l.shape, bf16),
            pltpu.VMEM((window * WIDTH, panels), f32),
            pltpu.VMEM((window * WIDTH, panels), bf16),
            pltpu.VMEM((leaves * WIDTH, panels), f32),
            pltpu.VMEM((leaves, panels, WIDTH), bf16),
            pltpu.VMEM((window, panels), f32),
            pltpu.VMEM((window, panels), f32),
            pltpu.VMEM((UNROLL, entries + -entries % 64, panels), f32),
            pltpu.VMEM((terms * 8, leaves * 8), f32),
            pltpu.VMEM((leaves, panels, panels), f32),
            pltpu.VMEM((leaves, padded, panels), f32),
            pltpu.SemaphoreType.DMA,
        ],
        compiler_params=params,
        name="main",
    )(
        counts, position, near_slots, far_slots,
        *pieces, far_offset, m2l, l2p, basis, gram,
    )

    def masks(axis):
        return [1 << power for power in range((lax.axis_size(axis) - 1).bit_length())]

    stages = [(0, bit if bit == 1 else bit | 1) for bit in masks("grp")]
    stages += [(bit, 1) for bit in masks("seg")]
    for stage in stages[:-1]:
        tile = tile + swap(tile, *stage)
    other = swap(tile, *stages[-1])

    return pl.pallas_call(
        final_kernel,
        out_shape=(
            jax.ShapeDtypeStruct((leaves, panels), f32),
            jax.ShapeDtypeStruct((krylov + 1,), f32),
        ),
        in_specs=smem(1) + anywhere(4),
        out_specs=tuple(vmem(2)),
        scratch_shapes=[pltpu.VMEM(a.shape, f32) for a in (basis, image, tile, other)]
        + [pltpu.SemaphoreType.DMA((4,))],
        compiler_params=small,
        name="final",
    )(counts, basis, image, tile, other)


def solution(mesh):
    placed = (
        P(None, ("seg", "grp"), None),
        P(("seg", "grp"), None, None),
        P(("seg", "grp"), None),
        P(("seg", "grp"), None, None),
        P(("seg", "grp"), None, None),
        P(),
        P(("seg", "grp")),
        P(("seg", "grp"), None),
        P(("seg", "grp"), None),
        P(("seg", "grp"), None),
    )
    return jax.shard_map(
        on_device,
        mesh=mesh,
        in_specs=placed,
        out_specs=(P(("seg", "grp"), None), P()),
        check_vma=False,
    )
```

```python
import functools

import jax
import jax.numpy as jnp
from jax import lax
from jax.experimental import pallas as pl
from jax.experimental.pallas import tpu as pltpu
from jax.sharding import PartitionSpec as P

four_pi = 12.566370614359172
epsilon = 1e-06
bf16 = jnp.bfloat16
f32 = jnp.float32
WIDTH = 16
CENTRE = 2.0
UNROLL = 8
LIMIT = 56 * 1024 * 1024

across = (((1,), (1,)), ((), ()))


def vmem(count):
    return [pl.BlockSpec(memory_space=pltpu.VMEM)] * count


def anywhere(count):
    return [pl.BlockSpec(memory_space=pl.ANY)] * count


def smem(count):
    return [pl.BlockSpec(memory_space=pltpu.SMEM)] * count


def live_rows(counts, shape):
    return (lax.broadcasted_iota(jnp.int32, shape, 0) < counts[0]).astype(f32)


def prep_kernel(counts, basis, coords, areas, p2m, block):
    leaves, panels = areas.shape
    terms = p2m.shape[0]
    current = basis[basis.shape[0] - 1] * live_rows(counts, (leaves, panels))
    rounded = current.astype(bf16).astype(f32)
    lane = lax.broadcasted_iota(jnp.int32, (leaves, panels), 1)
    poles = jnp.zeros((leaves, panels), f32)
    for k in range(terms):
        moved = jnp.sum(p2m[k].astype(f32) * rounded, axis=1, keepdims=True)
        poles = jnp.where(lane == k, moved, poles)
    for c in range(3):
        block[c] = coords[c]
    block[3] = areas[...]
    block[4] = areas[...] * current * (1.0 / four_pi)
    block[5] = poles


def slot_of(window, table, leaves, me, order_low):
    groups = len(table[0])
    span = groups * leaves
    low = (window < span).astype(jnp.int32)
    high = (window >= 2 * span).astype(jnp.int32)
    order = low * order_low + high * (3 - order_low)
    inner = window - span * (1 - low + high)
    group = jnp.zeros_like(window)
    for g in range(1, groups):
        group += (inner >= g * leaves).astype(jnp.int32)
    key = order * groups + (group ^ me)
    column = jnp.zeros_like(window)
    for i, line in enumerate(table):
        for j, at in enumerate(line):
            column = jnp.where(key == i * groups + j, at, column)
    return column * leaves + inner - group * leaves


def plan_kernel(table, counts, basis, near, far, near_slots, far_slots, gram):
    krylov, leaves, panels = basis.shape
    me = lax.axis_index("grp")
    order_low = 2 - lax.rem(lax.axis_index("seg"), 2)
    near_slots[...] = slot_of(near[...], table, leaves, me, order_low)
    far_slots[...] = slot_of(far[...], table, leaves, me, order_low)
    live = live_rows(counts, (leaves, panels))
    masked = [basis[j] * live for j in range(krylov)]
    lane = lax.broadcasted_iota(jnp.int32, (krylov, panels), 1)
    tile = jnp.zeros((krylov, panels), f32)
    for j in range(krylov):
        rows_j = [jnp.sum(masked[i] * masked[j], axis=0, keepdims=True) for i in range(krylov)]
        column = jnp.sum(jnp.concatenate(rows_j, axis=0), axis=1, keepdims=True)
        tile = jnp.where(lane == krylov + j, column, tile)
    population = (jnp.minimum(counts[0], leaves) * panels).astype(f32)
    gram[...] = jnp.where(lane == 2, population, tile)


def thirds(value):
    first = value.astype(bf16).astype(f32)
    second = (value - first).astype(bf16).astype(f32)
    return first, second, value - first - second


pairs = ((0, 0), (0, 1), (1, 0))


def main_kernel(orders, segments, *refs):
    pieces = len(orders)
    counts, near, far = refs[0:3]
    blocks = refs[3 : 3 + pieces]
    classes, m2l_hbm, l2p, basis, gram, image_out, tile_out = refs[3 + pieces : 10 + pieces]
    m2l, source32, source16, target32, target16 = refs[10 + pieces : 15 + pieces]
    charge, poles32, taken, sums, totals, found, sem = refs[15 + pieces :]
    krylov, leaves, panels = basis.shape
    terms = l2p.shape[0]
    offsets = m2l.shape[1]
    copy = pltpu.make_async_copy(m2l_hbm, m2l, sem)
    copy.start()
    segment = lax.axis_index("seg")
    low_end = jnp.where(segment >= 2, 1.0, 0.0)
    high_end = jnp.where(segment < segments - 2, 1.0, 0.0)
    inside = jnp.where(lax.rem(segment, 2) == 0, low_end, high_end)

    ones = jnp.ones((leaves, panels), f32)
    zeros = jnp.zeros((leaves, panels), f32)

    def lay(ref, base, rows):
        for k in range(WIDTH):
            value = rows[k] if k < len(rows) else zeros
            ref[pl.ds(base * WIDTH + k, leaves, stride=WIDTH), :] = value

    for b in range(pieces):
        got = blocks[b]
        point = [got[c] - CENTRE for c in range(3)]
        area = got[3]
        area = jnp.where(area > 0.0, area, 1.0)
        split = [thirds(p)[0:2] for p in point]
        square = point[0] * point[0] + point[1] * point[1] + point[2] * point[2]
        rows = [split[c][q] for c in range(3) for (_, q) in pairs]
        lay(source32, b * leaves, rows + list(thirds(square + area)) + [ones] * 3)
        if b == 0:
            rows = [split[c][p] * (-2.0) for c in range(3) for (p, _) in pairs]
            lay(target32, 0, rows + [ones] * 3 + list(thirds(square)))
        known = inside if orders[b] == 2 else 1.0
        charge[pl.ds(b * leaves, leaves), :] = got[4] * known
        poles32[pl.ds(b * leaves, leaves), :] = got[5] * known
    source16[...] = source32[...].astype(bf16)
    for leaf in range(leaves):
        target16[leaf] = target32[leaf * WIDTH : (leaf + 1) * WIDTH, :].T.astype(bf16)
    neighbours = near.shape[1]

    entries = far.shape[1]
    padded = found.shape[1]
    depth = taken.shape[1]
    taken[:, entries:, :] = jnp.zeros((taken.shape[0], depth - entries, panels), f32)

    def near_body(leaf, i):
        total = jnp.zeros((panels, panels), f32)
        for start in range(0, neighbours, 2):
            ids = [near[leaf, e] for e in range(start, min(start + 2, neighbours))]
            source = [source16[pl.ds(pl.multiple_of(s * WIDTH, WIDTH), WIDTH), :] for s in ids]
            source = jnp.concatenate(source, axis=1) if len(ids) > 1 else source[0]
            inverse = lax.rsqrt(jnp.dot(target16[leaf], source, preferred_element_type=f32))
            for e, s in enumerate(ids):
                total += inverse[:, e * panels : (e + 1) * panels] * charge[pl.ds(s, 1), :]
        totals[leaf] = total

    def far_gather(leaf, i):
        for e in range(entries):
            taken[i, e : e + 1, :] = poles32[pl.ds(far[leaf, e], 1), :]
        pole = taken[i]
        high = pole.astype(bf16)
        pole = jnp.concatenate([high, (pole - high.astype(f32)).astype(bf16)], axis=1)
        offset = classes[pl.ds(leaf, 1), :]
        by_class = lax.broadcasted_iota(jnp.int32, (padded, entries), 0) == offset
        by_class = jnp.concatenate(
            [by_class.astype(f32), jnp.zeros((padded, depth - entries), f32)], axis=1
        ).astype(bf16)
        both = jnp.dot(by_class, pole, preferred_element_type=f32)
        found[leaf] = both[:, 0:panels] + both[:, panels : 2 * panels]

    repeat(leaves, leaves, near_body)
    repeat(leaves, UNROLL, far_gather)
    nearby = jnp.concatenate(
        [jnp.sum(totals[leaf].T, axis=0, keepdims=True) for leaf in range(leaves)], axis=0
    )
    copy.wait()

    group = 8
    filler = jnp.zeros((terms * group, panels - terms), bf16)

    def translate(table, at):
        part = found[:, pl.ds(at, group), :].reshape(leaves * group, panels)
        first = part.astype(bf16)
        second = (part - first.astype(f32)).astype(bf16)
        table = jnp.concatenate([table.reshape(terms * group, terms), filler], axis=1)
        return lax.dot_general(
            jnp.concatenate([table, table], axis=1),
            jnp.concatenate([first, second], axis=1),
            across,
            preferred_element_type=f32,
        )

    full = offsets // group
    rest = offsets % group
    sums[...] = jnp.zeros_like(sums)
    if rest:
        tail = m2l[:, full * group : offsets, :].astype(f32)
        tail = jnp.concatenate([tail, jnp.zeros((terms, group - rest, terms), f32)], axis=1)
        sums[...] = translate(tail.reshape(terms * group, terms).astype(bf16), full * group)
    batch = next(n for n in range(min(39, full), 0, -1) if full % n == 0)

    def far_body(step, carry):
        value = None
        for i in range(batch):
            at = pl.multiple_of((step * batch + i) * group, group)
            one = translate(m2l[:, pl.ds(at, group), :], at)
            value = one if value is None else value + one
        sums[...] += value
        return carry

    lax.fori_loop(0, full // batch, far_body, 0)
    spread = leaves * group
    row = lax.broadcasted_iota(jnp.int32, (terms * group, spread), 0) & (group - 1)
    lane = lax.broadcasted_iota(jnp.int32, (terms * group, spread), 1) & (group - 1)
    kept = jnp.where(row == lane, sums[...], 0.0)
    kept = jnp.sum(kept.reshape(terms, group, spread), axis=1)
    owner = lax.broadcasted_iota(jnp.int32, (leaves, spread), 0) * group
    lane = lax.broadcasted_iota(jnp.int32, (leaves, spread), 1)
    pick = ((lane >= owner) & (lane < owner + group)).astype(f32).astype(bf16)
    local = jnp.zeros((leaves, terms), f32)
    for part in thirds(kept):
        local += lax.dot_general(pick, part.astype(bf16), across, preferred_element_type=f32)
    local = local.astype(bf16).astype(f32)
    distant = zeros
    for k in range(terms):
        distant += l2p[k].astype(f32) * local[:, k : k + 1]

    live = live_rows(counts, (leaves, panels))
    current = basis[krylov - 1] * live
    image = (0.5 * current + nearby + distant) * live
    image_out[...] = image
    rows = [jnp.sum(basis[j] * live * image, axis=0, keepdims=True) for j in range(krylov)]
    product = jnp.sum(jnp.concatenate(rows, axis=0), axis=1, keepdims=True)
    energy = jnp.sum(jnp.sum(image * image, axis=0, keepdims=True), axis=1, keepdims=True)
    lane = lax.broadcasted_iota(jnp.int32, (krylov, panels), 1)
    tile_out[...] = jnp.where(lane == 0, product, jnp.where(lane == 1, energy, gram[...]))


def repeat(count, most, body):
    batch = next(n for n in range(most, 0, -1) if count % n == 0)

    def several(step, carry):
        for i in range(batch):
            body(step * batch + i, i)
        return carry

    lax.fori_loop(0, count // batch, several, 0)


def final_kernel(counts, *refs):
    vector, column = refs[4:6]
    basis, image, tile, other = refs[6:10]
    sems = refs[10]
    copies = [pltpu.make_async_copy(refs[i], refs[6 + i], sems.at[i]) for i in range(4)]
    for copy in copies:
        copy.start()
    for copy in copies:
        copy.wait()
    krylov, leaves, panels = basis.shape
    sums = tile[...] + other[...]
    population = sums[0:1, 2:3]
    energy = sums[0:1, 1:2]
    products = sums[:, 0:1]
    coefficients = products / population
    row = lax.broadcasted_iota(jnp.int32, (krylov, panels), 0)
    lane = lax.broadcasted_iota(jnp.int32, (krylov, panels), 1)
    in_gram = (lane >= krylov) & (lane < 2 * krylov)
    applied = jnp.sum(jnp.where(in_gram, coefficients * sums, 0.0), axis=0, keepdims=True)
    across_lanes = jnp.sum(jnp.where(lane == krylov + row, coefficients, 0.0), axis=0, keepdims=True)
    curvature = jnp.sum(applied * across_lanes, axis=1, keepdims=True)
    crossed = jnp.sum(coefficients * products, axis=0, keepdims=True)
    squares = energy - 2.0 * crossed + curvature
    scale = jnp.sqrt(squares / population + epsilon)
    live = live_rows(counts, (leaves, panels))
    residue = image[...]
    for j in range(krylov):
        residue = residue - coefficients[j : j + 1, 0:1] * (basis[j] * live)
    vector[...] = residue / scale
    placed = jnp.sum(jnp.where(lane == row, coefficients, 0.0), axis=0, keepdims=True)
    placed = jnp.where(lane[0:1] == krylov, scale, placed)
    column[...] = placed.reshape(panels)[0 : krylov + 1]


def move(value, step):
    segments, groups = lax.axis_size("seg"), lax.axis_size("grp")
    moves = []
    for segment in range(segments):
        for group in range(groups):
            to = step(segment, group)
            moves.append((segment * groups + group, to[0] * groups + to[1]))
    return lax.ppermute(value, ("seg", "grp"), moves)


def swap(value, segment_bit, group_bit):
    return move(value, lambda s, g: (s ^ segment_bit, g ^ group_bit))


def hop(value):
    segments = lax.axis_size("seg")

    def step(s, g):
        to = s + 2 if s % 2 == 0 else s - 2
        return (to if 0 <= to < segments else s ^ 1, g ^ 1)

    return move(value, step)


def on_device(basis, coords, areas, p2m, l2p, m2l, counts, near_list, far_list, far_offset):
    krylov, leaves, panels = basis.shape
    coords = jnp.transpose(coords, (1, 0, 2))
    p2m = jnp.transpose(p2m, (1, 0, 2))
    l2p = jnp.transpose(l2p, (2, 0, 1))
    m2l = jnp.transpose(m2l, (1, 0, 2))
    terms, offsets = m2l.shape[:2]
    groups = lax.axis_size("grp")
    params = pltpu.CompilerParams(vmem_limit_bytes=LIMIT)
    small = pltpu.CompilerParams(vmem_limit_bytes=LIMIT // 8)
    block = pl.pallas_call(
        prep_kernel,
        out_shape=jax.ShapeDtypeStruct((6, leaves, panels), f32),
        in_specs=smem(1) + vmem(4),
        out_specs=pl.BlockSpec(memory_space=pltpu.VMEM),
        compiler_params=params,
        name="prep",
    )(counts, basis, coords, areas, p2m)

    window = 3 * groups * leaves
    entries = far_list.shape[1]
    padded = offsets + -offsets % 16

    def spread(pieces):
        bit = 2
        while bit < groups:
            pieces = pieces + [swap(v, 0, bit | 1) for v in pieces]
            bit *= 2
        return pieces

    beside = swap(block, 1, 1)
    own = spread([block])
    rels = [0]
    bit = 2
    while bit < groups:
        rels = rels + [rel ^ bit ^ 1 for rel in rels]
        bit *= 2
    keys = [(0, rel) for rel in rels] + [(1, rel ^ 1) for rel in rels] + [(2, rel) for rel in rels]
    keys = keys + [(order, rel ^ 1) for order, rel in keys]
    table = [[keys.index((order, rel)) for rel in range(groups)] for order in range(3)]
    near_slots, far_slots, gram = pl.pallas_call(
        functools.partial(plan_kernel, table),
        out_shape=(
            jax.ShapeDtypeStruct(near_list.shape, jnp.int32),
            jax.ShapeDtypeStruct(far_list.shape, jnp.int32),
            jax.ShapeDtypeStruct((krylov, panels), f32),
        ),
        in_specs=smem(1) + vmem(3),
        out_specs=tuple(vmem(3)),
        compiler_params=params,
        name="plan",
    )(counts, basis, near_list, far_list)

    beside, near_slots = lax.optimization_barrier((beside, near_slots))
    beyond = hop(beside)
    pieces = own + [beside] + [swap(v, 1, 1) for v in own[1:]] + spread([beyond])
    pieces = pieces + [swap(v, 0, 1) for v in pieces]

    image, tile = pl.pallas_call(
        functools.partial(main_kernel, [order for order, _ in keys], lax.axis_size("seg")),
        out_shape=(
            jax.ShapeDtypeStruct((leaves, panels), f32),
            jax.ShapeDtypeStruct((krylov, panels), f32),
        ),
        in_specs=smem(3) + vmem(len(pieces) + 1) + anywhere(1) + vmem(3),
        out_specs=tuple(vmem(2)),
        scratch_shapes=[
            pltpu.VMEM(m2l.shape, bf16),
            pltpu.VMEM((window * WIDTH, panels), f32),
            pltpu.VMEM((window * WIDTH, panels), bf16),
            pltpu.VMEM((leaves * WIDTH, panels), f32),
            pltpu.VMEM((leaves, panels, WIDTH), bf16),
            pltpu.VMEM((window, panels), f32),
            pltpu.VMEM((window, panels), f32),
            pltpu.VMEM((UNROLL, entries + -entries % 64, panels), f32),
            pltpu.VMEM((terms * 8, leaves * 8), f32),
            pltpu.VMEM((leaves, panels, panels), f32),
            pltpu.VMEM((leaves, padded, panels), f32),
            pltpu.SemaphoreType.DMA,
        ],
        compiler_params=params,
        name="main",
    )(
        counts, near_slots, far_slots,
        *pieces, far_offset, m2l, l2p, basis, gram,
    )

    def masks(axis):
        return [1 << power for power in range((lax.axis_size(axis) - 1).bit_length())]

    stages = [(0, bit if bit == 1 else bit | 1) for bit in masks("grp")]
    stages += [(bit, 1) for bit in masks("seg")]
    for stage in stages[:-1]:
        tile = tile + swap(tile, *stage)
    other = swap(tile, *stages[-1])

    return pl.pallas_call(
        final_kernel,
        out_shape=(
            jax.ShapeDtypeStruct((leaves, panels), f32),
            jax.ShapeDtypeStruct((krylov + 1,), f32),
        ),
        in_specs=smem(1) + anywhere(4),
        out_specs=tuple(vmem(2)),
        scratch_shapes=[pltpu.VMEM(a.shape, f32) for a in (basis, image, tile, other)]
        + [pltpu.SemaphoreType.DMA((4,))],
        compiler_params=small,
        name="final",
    )(counts, basis, image, tile, other)


def solution(mesh):
    placed = (
        P(None, ("seg", "grp"), None),
        P(("seg", "grp"), None, None),
        P(("seg", "grp"), None),
        P(("seg", "grp"), None, None),
        P(("seg", "grp"), None, None),
        P(),
        P(("seg", "grp")),
        P(("seg", "grp"), None),
        P(("seg", "grp"), None),
        P(("seg", "grp"), None),
    )
    return jax.shard_map(
        on_device,
        mesh=mesh,
        in_specs=placed,
        out_specs=(P(("seg", "grp"), None), P()),
        check_vma=False,
    )
```
